32 devices in a mesh: groups: 2 (over y), rows: 4 (over x, core), cols: 4 (over z).
Axes of the slice: x: 2, y: 2, z: 4, core: 2. Of those that a mesh axis runs over, the one named last changes fastest.
Arguments:
- block_values: bfloat16 [192, 8, 128, 128], P(('groups', 'rows'), 'cols'), parts along dimension 0, may hold values from -3 to 3
- block_columns: int32 [192, 8], P(('groups', 'rows'), 'cols'), parts along dimension 0, may hold values from -1 to 95, as said below
- product_columns: int32 [192, 16], P(('groups', 'rows'), 'cols'), parts along dimension 0, may hold values from -1 to 95, as said below
Outputs:
- square: float32 [192, 16, 128, 128], P(('groups', 'rows'), 'cols'), parts along dimension 0
The draws below stay inside these ranges and needn't reach their ends.
There are 2 independent parts, one for each index of `groups`. The reference program is written for one: setup_inputs(seed, part) draws one part's arguments, and reference() takes and returns one part's arrays. A program takes and returns all parts, laid end to end along the dimension named above; each array names one. Nothing has to cross between parts.
Inputs may be any that keep to these rules, and one draw needn't show every extreme that they name: `block_columns`: within a block row the stored columns are distinct and lie in i to i + 9 for block row i; slot 0 is the diagonal; a slot is -1 exactly where its column would pass the last block row. `product_columns`: within a block row the columns are distinct and lie in i to i + 2 * 10 - 2 for block row i; slot 0 is the diagonal; a slot is -1 exactly where its column would pass the last block row.
All inputs are finite; a program needn't handle non-finite values.
Results may differ from the reference program's by a relative error of at most 0.0003.
Values may be sent and summed in bfloat16 or wider, within the bound.
No kernel may reach another device: no remote copies, remote signals or barrier semaphores. Data moves between devices by JAX's collectives and lax.ppermute only.
A program may use at most 320 MiB of HBM per device.

```python
import jax
import jax.numpy as jnp
from jax import lax

TILE = 128
W = 10
S = 8
SO = 16
BR = 24
NB = 96


def row_offsets(key, count, span):
    keys = jax.random.split(key, NB)

    def one_row(row_key):
        return jax.random.permutation(row_key, span)[:count]
    return jax.vmap(one_row)(keys).astype(jnp.int32)


def bounded_columns(offsets):
    column_ids = jnp.arange(NB, dtype=jnp.int32)[:, None] + offsets
    return jnp.where(column_ids < NB, column_ids, -1).astype(jnp.int32)


def draw_block_columns(key, part):
    key = jax.random.fold_in(key, 11)
    others = row_offsets(key, S - 1, W - 1) + 1
    offsets = jnp.concatenate([jnp.zeros((NB, 1), jnp.int32), others], axis=1)
    return bounded_columns(offsets)


def draw_product_columns(key, part):
    key = jax.random.fold_in(key, 23)
    others = row_offsets(key, SO - 1, 2 * W - 2) + 1
    offsets = jnp.concatenate([jnp.zeros((NB, 1), jnp.int32), others], axis=1)
    return bounded_columns(offsets)


def level_of(stream_key, dims, shards, low, high):
    def one(position, blocks):
        draws = jax.random.uniform(jax.random.fold_in(jax.random.fold_in(stream_key, 6), position), (blocks,), jnp.float32, low / len(shards), high / len(shards))
        return jnp.repeat(jnp.exp(draws), dims[position] // blocks).reshape((-1,) + (1,) * (len(dims) - position - 1))

    factor_of = one(*shards[0])
    for cut in shards[1:]:
        factor_of = factor_of * one(*cut)
    return factor_of


def noise(own_key, dims, scale, most, cuts=(), kind=jnp.bfloat16):
    drawn = scale * jax.random.normal(own_key, dims, jnp.float32)
    if cuts:
        drawn = drawn * level_of(own_key, dims, cuts, -0.22, 0.18)
    return jnp.clip(drawn, -most, most).astype(kind)


def setup_inputs(seed: int = 0, part: int = 0) -> dict:
    streams_of = jax.random.split(jax.random.key(seed), 4)
    part_splits = jax.random.split(jax.random.fold_in(streams_of[3], part), 4)
    block_values = noise(part_splits[0], (NB, S, TILE, TILE), 0.2, 3.0, ((0, 4), (1, 4)))
    block_columns = draw_block_columns(jax.random.fold_in(jax.random.fold_in(streams_of[3], part), 71), part)
    product_columns = draw_product_columns(jax.random.fold_in(jax.random.fold_in(streams_of[3], part), 71), part)
    return dict(block_values=block_values, block_columns=block_columns, product_columns=product_columns)


def make_band(values, columns, row_ids):
    offsets = columns - row_ids[:, None]
    reach = jnp.arange(W, dtype=jnp.int32)
    band_tiles = jnp.zeros((values.shape[0], W, values.shape[2], values.shape[3]), values.dtype)
    for slot_index in range(values.shape[1]):
        picked = (offsets[:, slot_index, None] == reach[None, :]) & (columns[:, slot_index, None] >= 0)
        band_tiles = jnp.where(picked[:, :, None, None], values[:, slot_index, None], band_tiles)
    diagonal = band_tiles[:, 0]
    diagonal = jnp.triu(diagonal) + jnp.swapaxes(jnp.triu(diagonal, 1), 1, 2)
    return band_tiles.at[:, 0].set(diagonal)


def block_product(band_tiles, wanted, first_row, row_count):
    lead_rows = W - 1
    ext_count = band_tiles.shape[0]
    global_rows = first_row + jnp.arange(row_count, dtype=jnp.int32)
    distance = jnp.where(wanted >= 0, wanted - global_rows[:, None], -4 * W).astype(jnp.int32)
    local_rows = jnp.arange(row_count, dtype=jnp.int32)[:, None]
    total_sum = jnp.zeros((row_count, wanted.shape[1], TILE, TILE), jnp.float32)
    for step_k in range(-(W - 1), W):
        if step_k >= 0:
            left_tile = band_tiles[lead_rows + step_k:lead_rows + step_k + row_count, step_k]
        else:
            left_tile = jnp.swapaxes(band_tiles[lead_rows + step_k:lead_rows + step_k + row_count, -step_k], 1, 2)
        reach = distance - step_k
        holder = lead_rows + step_k + local_rows
        upper_part = band_tiles[holder, jnp.clip(reach, 0, W - 1)]
        lower_rows = jnp.clip(holder + reach, 0, ext_count - 1)
        lower_part = jnp.swapaxes(band_tiles[lower_rows, jnp.clip(-reach, 0, W - 1)], 2, 3)
        upper_ok = ((reach >= 0) & (reach < W))[:, :, None, None]
        lower_ok = ((reach < 0) & (reach > -W))[:, :, None, None]
        right_tile = jnp.where(upper_ok, upper_part, jnp.where(lower_ok, lower_part, jnp.zeros((), band_tiles.dtype)))
        total_sum = total_sum + jnp.einsum("rab,rqbc->rqac", left_tile.astype(jnp.float32), right_tile.astype(jnp.float32), precision=lax.Precision.HIGHEST)
    return total_sum


def reference(block_values, block_columns, product_columns):
    total_rows = block_values.shape[0]
    band_tiles = make_band(block_values, block_columns, jnp.arange(total_rows, dtype=jnp.int32))
    band_tiles = jnp.pad(band_tiles, ((W - 1, 2 * W - 2), (0, 0), (0, 0), (0, 0)))
    starts = jnp.arange(total_rows // BR, dtype=jnp.int32) * BR

    def one_block(start):
        piece = lax.dynamic_slice_in_dim(band_tiles, start, BR + 3 * W - 3, 0)
        wanted = lax.dynamic_slice_in_dim(product_columns, start, BR, 0)
        return block_product(piece, wanted, start, BR)

    result = lax.map(one_block, starts)
    return result.reshape(total_rows, product_columns.shape[1], TILE, TILE)
```

```python
import functools

import jax
import jax.numpy as jnp
from jax import lax
from jax.experimental import pallas as pl
from jax.experimental.pallas import tpu as pltpu
from jax.sharding import PartitionSpec as P

W = 10
LEAD = W - 1
SPAN = 2 * W - 1
UNROLL = 4
BITS = 10
MASK = (1 << BITS) - 1


def up_pairs(size, step):
    return [(i, i + 1) for i in range(step - 1, size - 1)]


def down_pairs(size, step):
    return [(i + 1, i) for i in range(size - step)]


def row_shift(array, by):
    size = lax.axis_size("rows")
    return lax.ppermute(array, "rows", [(i, i + by) for i in range(size) if 0 <= i + by < size])


def factor_table(columns, first_row, row_count):
    total, slots = columns.shape
    ext = row_count + 2 * LEAD
    padded = jnp.pad(columns, ((LEAD, LEAD), (0, 0)), constant_values=-1)
    here = lax.dynamic_slice_in_dim(padded, first_row, ext, 0)
    row_ids = first_row - LEAD + jnp.arange(ext, dtype=jnp.int32)
    offsets = jnp.where(here >= 0, here - row_ids[:, None], -1)
    reach = jnp.arange(W, dtype=jnp.int32)
    slot_ids = jnp.arange(slots, dtype=jnp.int32)
    index = jnp.arange(ext, dtype=jnp.int32)[:, None] * slots + slot_ids[None, :]
    picked = offsets[:, :, None] == reach[None, None, :]
    upper = jnp.max(jnp.where(picked, index[:, :, None], -1), axis=1)
    lower = jnp.where(upper >= 0, upper + ext * slots, -1)
    parts = []
    for m in range(LEAD, 0, -1):
        parts.append(jnp.pad(lower[: ext - m, m], (m, 0), constant_values=-1)[:, None])
    return jnp.concatenate(parts + [upper], axis=1)


def list_kernel(row_count, slot_count, zero_id, first_ref, table_ref, wanted_ref, left_ref, right_ref, count_ref):
    first = first_ref[0]

    def per_output(out_id, base):
        row = out_id // slot_count
        slot = out_id - row * slot_count
        want = wanted_ref[row, slot]
        distance = want - first - row
        start = jnp.where(want >= 0, distance - LEAD, W)

        def per_step(step, count):
            left = table_ref[row + LEAD + jnp.maximum(step, 0), step + LEAD]
            right = table_ref[row + LEAD + step, distance - step + LEAD]
            valid = (left >= 0) & (right >= 0)
            at = base + count // 2

            @pl.when(valid & (count % 2 == 0))
            def _():
                left_ref[at] = left | (zero_id << BITS)
                right_ref[at] = right | (zero_id << BITS) | (out_id << (2 * BITS))

            @pl.when(valid & (count % 2 == 1))
            def _():
                left_ref[at] = (left_ref[at] & MASK) | (left << BITS)
                right_ref[at] = (right_ref[at] & ~(MASK << BITS)) | (right << BITS)

            return count + valid.astype(jnp.int32)

        count = lax.fori_loop(start, W, per_step, jnp.int32(0))
        return base + (count + 1) // 2

    total = lax.fori_loop(0, row_count * slot_count, per_output, jnp.int32(0))
    for extra in range(UNROLL):
        left_ref[total + extra] = zero_id | (zero_id << BITS)
        right_ref[total + extra] = zero_id | (zero_id << BITS)
    count_ref[0] = (total + UNROLL - 1) // UNROLL


def product_kernel(plan, out_count, ext, slots, here_ref, left_ref, right_ref, count_ref, *refs):
    count = len(plan)
    pieces, out_ref, blocks, sem = refs[:count], refs[count], refs[count + 1], refs[count + 2]
    cols = here_ref[1]
    me = here_ref[0]
    stored = ext * slots

    def copies(go):
        for n, (piece, (rows, shift)) in enumerate(zip(pieces, plan)):
            own = piece.shape[1]
            owner = me + shift

            @pl.when((owner >= 0) & (owner < cols))
            def _(piece=piece, rows=rows, owner=owner, own=own):
                for r in range(piece.shape[0]):
                    go(pltpu.make_async_copy(piece.at[r], blocks.at[pl.ds((rows + r) * slots + owner * own, own)], sem))

    copies(lambda c: c.start())
    out_ref[...] = jnp.zeros_like(out_ref)
    blocks[2 * stored] = jnp.zeros(blocks.shape[1:], blocks.dtype)
    copies(lambda c: c.wait())

    def turn(row, _):
        at = row * slots
        tile = blocks[at]
        a = lax.broadcasted_iota(jnp.int32, tile.shape, 0)
        b = lax.broadcasted_iota(jnp.int32, tile.shape, 1)
        wide = tile.astype(jnp.float32)
        whole = jnp.where(a <= b, wide, wide.T).astype(tile.dtype)
        blocks[at] = whole
        blocks[stored + at] = whole
        for s in range(1, slots):
            blocks[stored + at + s] = blocks[at + s].T
        return 0

    lax.fori_loop(0, ext, turn, 0)

    def multiply(group, _):
        sums = []
        for u in range(UNROLL):
            left = left_ref[group * UNROLL + u]
            right = right_ref[group * UNROLL + u]
            lhs = jnp.concatenate([blocks[left & MASK], blocks[left >> BITS]], axis=1)
            rhs = jnp.concatenate([blocks[right & MASK], blocks[(right >> BITS) & MASK]], axis=0)
            sums.append((right >> (2 * BITS), jnp.dot(lhs, rhs, preferred_element_type=jnp.float32)))
        for at, value in sums:
            out_ref[at] += value
        return 0

    lax.fori_loop(0, count_ref[0], multiply, 0)


def body(block_values, block_columns, product_columns):
    row_count, own, tile, _ = block_values.shape
    size = lax.axis_size("cols")
    slots = size * own
    wanted_slots = product_columns.shape[1]
    ext = row_count + 2 * LEAD
    first_row = lax.axis_index("rows") * row_count
    me = lax.axis_index("cols")

    spans = [(0, LEAD), (row_count - LEAD, row_count), (LEAD, row_count - LEAD)]
    plan, pieces = [], []

    def keep(array, rows, shift):
        plan.append((rows, shift))
        pieces.append(array)

    def halo(part, array, shift):
        if part == 0:
            keep(row_shift(array, -1), LEAD + row_count, shift)
        if part == 1:
            keep(row_shift(array, 1), 0, shift)

    going_up = [block_values[a:b] for a, b in spans]
    going_down = list(going_up)
    keep(block_values, LEAD, 0)
    halo(0, going_up[0], 0)
    halo(1, going_up[1], 0)
    for step in range(1, size):
        for part, (start, _) in enumerate(spans):
            going_up[part] = lax.ppermute(going_up[part], "cols", up_pairs(size, step))
            going_down[part] = lax.ppermute(going_down[part], "cols", down_pairs(size, step))
            keep(going_up[part], LEAD + start, -step)
            keep(going_down[part], LEAD + start, step)
            halo(part, going_up[part], -step)
            halo(part, going_down[part], step)

    columns = lax.all_gather(block_columns, ("rows", "cols"), axis=0)
    columns = columns.reshape(-1, size, row_count, own).swapaxes(1, 2).reshape(-1, slots)
    table = factor_table(columns, first_row, row_count)

    smem = pl.BlockSpec(memory_space=pltpu.SMEM)
    out_count = row_count * wanted_slots
    cap = out_count * W + UNROLL
    zero_id = 2 * ext * slots
    left, right, count = pl.pallas_call(
        functools.partial(list_kernel, row_count, wanted_slots, zero_id),
        out_shape=[jax.ShapeDtypeStruct((cap,), jnp.int32)] * 2 + [jax.ShapeDtypeStruct((1,), jnp.int32)],
        in_specs=[smem] * 3,
        out_specs=[smem] * 3,
    )(first_row.reshape(1), table, product_columns)

    out = pl.pallas_call(
        functools.partial(product_kernel, tuple(plan), out_count, ext, slots),
        out_shape=jax.ShapeDtypeStruct((out_count, tile, tile), jnp.float32),
        in_specs=[smem] * 4 + [pl.BlockSpec(memory_space=pl.ANY)] * len(pieces),
        out_specs=pl.BlockSpec(memory_space=pltpu.VMEM),
        scratch_shapes=[
            pltpu.VMEM((2 * ext * slots + 1, tile, tile), block_values.dtype),
            pltpu.SemaphoreType.DMA,
        ],
        compiler_params=pltpu.CompilerParams(vmem_limit_bytes=48 << 20),
    )(jnp.stack([me, jnp.int32(size)]), left, right, count, *pieces)
    return out.reshape(row_count, wanted_slots, tile, tile)


def solution(mesh):
    placed = (
        P(("groups", "rows"), "cols", None, None),
        P(("groups", "rows"), "cols"),
        P(("groups", "rows"), "cols"),
    )
    return jax.shard_map(
        body,
        mesh=mesh,
        in_specs=placed,
        out_specs=P(("groups", "rows"), "cols", None, None),
        check_vma=False,
    )
```

```python
import functools

import jax
import jax.numpy as jnp
from jax import lax
from jax.experimental import pallas as pl
from jax.experimental.pallas import tpu as pltpu
from jax.sharding import PartitionSpec as P

W = 10
LEAD = W - 1
SPAN = 2 * W - 1
WIDE = 4 * W
UNROLL = 16
BITS = 10
MASK = (1 << BITS) - 1
OUT_MASK = 127
STAGE_BIT = 27
STAGES = 5
ABSENT = 7
CHUNKS = 4
TABLE = 1024
WEIGHTS = {0: 1, 1: 1, 2: 1, 3: 1 << 33, 4: 1}
LIST_WEIGHT = 1

SMEM = pl.BlockSpec(memory_space=pltpu.SMEM)
VMEM = pl.BlockSpec(memory_space=pltpu.VMEM)
HBM = pl.BlockSpec(memory_space=pltpu.HBM)
ANY = pl.BlockSpec(memory_space=pl.ANY)
SMALL = pltpu.CompilerParams(vmem_limit_bytes=1 << 20)


def stage_of(step, last, edge):
    if step == last and step > 1:
        return 2 + edge
    if edge == 2:
        return 0 if step == 0 else 1
    return 0 if step <= 1 else 1


def quick(weight):
    return pl.CostEstimate(flops=weight, bytes_accessed=weight, transcendentals=0)


def up_pairs(size, step):
    return [(i, i + 1) for i in range(step - 1, size - 1)]


def down_pairs(size, step):
    return [(i + 1, i) for i in range(size - step)]


def row_shift(array, by):
    size = lax.axis_size("rows")
    return lax.ppermute(array, "rows", [(i, i + by) for i in range(size) if 0 <= i + by < size])


def segment_size(part_rows, slot_count):
    most = part_rows * (slot_count * (SPAN + 1) - slot_count * (slot_count - 1) // 2) + 4 * UNROLL
    return -(-most // 256) * 256


def list_kernel(
    row_count,
    own,
    slot_count,
    size,
    total_rows,
    place_ref,
    wanted_ref,
    columns_hbm,
    terms_ref,
    count_ref,
    table_ref,
    at_ref,
    columns_ref,
    sem,
):
    me, first = place_ref[0], place_ref[1]
    slots = size * own
    ext = row_count + 2 * LEAD
    stored = ext * slots
    zero_id = 2 * stored
    part = row_count // CHUNKS
    segment = segment_size(part, slot_count)
    junk = STAGES * CHUNKS * segment
    zero_term = zero_id | (zero_id << BITS)
    spare = WIDE - 1
    absent = ABSENT << STAGE_BIT
    here = first // row_count
    holders = total_rows // row_count

    def fetch(go):
        for near in range(3):
            holder = jnp.clip(here + near - 1, 0, holders - 1)
            source = pl.ds(pl.multiple_of(holder * size * TABLE, TABLE), size * TABLE)
            go(pltpu.make_async_copy(columns_hbm.at[source], columns_ref.at[pl.ds(near * size * TABLE, size * TABLE)], sem))

    fetch(lambda c: c.start())

    def clear(e, _):
        for c in range(WIDE - 1):
            table_ref[e * WIDE + c] = absent
        return 0

    lax.fori_loop(0, ext, clear, 0)

    stages = []
    for k in range(size):
        distance = jnp.abs(k - me)
        picks = []
        for edge in range(3):
            stage = jnp.int32(0)
            for step in range(size):
                stage = jnp.where(distance == step, stage_of(step, size - 1, edge), stage)
            picks.append(stage << STAGE_BIT)
        stages.append(picks)
    fetch(lambda c: c.wait())

    def enter(e, row_id, near, local, stage):
        line = e * WIDE + LEAD
        for k in range(size):
            for s in range(own):
                column = columns_ref[local + ((near * size + k) * TABLE + s * row_count)]
                reach = column - row_id
                good = (column >= 0) & (reach >= 0) & (reach < W)
                code = (e * slots + (k * own + s)) + stage(k)
                table_ref[jnp.where(good, line + reach, spare)] = code
                low = good & (reach > 0) & (e + reach < ext)
                table_ref[jnp.where(low, line + reach * (WIDE - 1), spare)] = code + stored

    @pl.when(first > 0)
    def _():
        def enter_before(r, _):
            at = row_count - LEAD + r
            enter(r, first - LEAD + r, 0, at, lambda k: stages[k][2])
            return 0

        lax.fori_loop(0, LEAD, enter_before, 0)

    def enter_own(r, _):
        edge = (r < LEAD) | (r >= row_count - LEAD)
        enter(r + LEAD, first + r, 1, r, lambda k: jnp.where(edge, stages[k][0], stages[k][1]))
        return 0

    lax.fori_loop(0, row_count, enter_own, 0)

    @pl.when(first + row_count < total_rows)
    def _():
        def enter_after(r, _):
            enter(LEAD + row_count + r, first + row_count + r, 2, r, lambda k: stages[k][2])
            return 0

        lax.fori_loop(0, LEAD, enter_after, 0)

    table_ref[spare] = absent

    lanes = range(CHUNKS)
    lines = ABSENT + 1
    for chunk in lanes:
        for stage in range(STAGES):
            at_ref[chunk * lines + stage] = (stage * CHUNKS + chunk) * segment

    def per_output(number, _):
        local = number // slot_count
        slot = number - local * slot_count
        rows = [chunk * part + local for chunk in lanes]
        wants = [wanted_ref[slot, row] for row in rows]
        distances = [jnp.where(want >= 0, want - first - row, SPAN) for want, row in zip(wants, rows)]
        tags = [(row * slot_count + slot) << (2 * BITS) for row in rows]
        bases = [(row + LEAD) * WIDE + LEAD for row in rows]
        rights_at = [base + d for base, d in zip(bases, distances)]
        for chunk in lanes:
            at_ref[chunk * lines + ABSENT] = junk
        for step in range(-LEAD, W):
            lefts = [table_ref[base + (max(step, 0) * WIDE + step)] for base in bases]
            rights = [table_ref[at + step * (WIDE - 1)] for at in rights_at]
            spots = [
                (jnp.maximum(left, right) >> STAGE_BIT) + chunk * lines
                for chunk, left, right in zip(lanes, lefts, rights)
            ]
            places = [at_ref[spot] for spot in spots]
            for chunk in lanes:
                terms_ref[places[chunk]] = lefts[chunk] + (rights[chunk] << BITS) + tags[chunk]
            for chunk in lanes:
                at_ref[spots[chunk]] = places[chunk] + 1
        for chunk in lanes:
            places = [at_ref[chunk * lines + stage] for stage in range(STAGES)]
            for stage in range(STAGES):
                terms_ref[places[stage]] = zero_term + tags[chunk]
                at_ref[chunk * lines + stage] = places[stage] + (places[stage] & 1)
        return 0

    lax.fori_loop(0, part * slot_count, per_output, 0)

    for stage in range(STAGES):
        for chunk in lanes:
            at = at_ref[chunk * lines + stage]
            tag = (chunk * part * slot_count) << (2 * BITS)
            for extra in range(2 * UNROLL):
                terms_ref[at + extra] = zero_term + tag
            used = at - (stage * CHUNKS + chunk) * segment
            count_ref[stage * CHUNKS + chunk] = (used + 2 * UNROLL - 1) // (2 * UNROLL)


def stage_kernel(stage, plan, ext, size, own, segment, place_ref, *refs):
    count = len(plan)
    first, final = stage == 0, stage == STAGES - 1
    count_ref, terms_hbm = refs[:2]
    pieces = refs[2 : count + 2]
    blocks, sums, out_ref, sem, terms_ref, list_sem = refs[count + (2 if first else 4) :]
    if not final:
        out_ref[0] = 0
    slots = size * own
    stored = ext * slots
    me = place_ref[0]

    def each(go):
        for piece, (source, rows, target, shift) in zip(pieces, plan):
            owner = me + (shift if not isinstance(shift, tuple) else jnp.where(me >= shift[0], -shift[0], shift[0]))

            @pl.when((owner >= 0) & (owner < size))
            def _(piece=piece, source=source, rows=rows, target=target, owner=owner):
                go(piece, source, rows, target, owner)

    shelf = blocks.reshape(blocks.shape[0] // slots, slots, *blocks.shape[1:])

    def copy(piece, source, rows, target, owner):
        return pltpu.make_async_copy(
            piece.at[pl.ds(source, rows)], shelf.at[pl.ds(target, rows), pl.ds(owner * own, own)], sem
        )

    def turn(piece, source, rows, target, owner):
        pace = max(n for n in range(1, 10) if rows % n == 0)

        def some(group, _):
            base = (target + group * pace) * slots + owner * own
            for r in range(pace):
                for s in range(own):
                    at = base + r * slots + s
                    blocks[stored + at] = blocks[at].T
            return 0

        lax.fori_loop(0, rows // pace, some, 0)

        def mirror(group, _):
            spots = [(target + group * 3 + r) * slots for r in range(3)]
            found = []
            for at in spots:
                tile, turned = blocks[at], blocks[stored + at]
                a = lax.broadcasted_iota(jnp.int32, tile.shape, 0)
                b = lax.broadcasted_iota(jnp.int32, tile.shape, 1)
                found.append(jnp.where(a <= b, tile, turned))
            for at, whole in zip(spots, found):
                blocks[at] = whole
                blocks[stored + at] = whole
            return 0

        @pl.when(owner == 0)
        def _():
            lax.fori_loop(0, rows // 3, mirror, 0)

    listing = pltpu.make_async_copy(
        terms_hbm.at[pl.ds(stage * CHUNKS * segment, CHUNKS * segment)], terms_ref, list_sem
    )
    listing.start()
    each(lambda *what: copy(*what).start())
    if first:
        blocks[2 * stored] = jnp.zeros(blocks.shape[1:], blocks.dtype)
        sums[...] = jnp.zeros_like(sums)
    each(lambda *what: copy(*what).wait())
    each(turn)
    listing.wait()

    part = sums.shape[0] // CHUNKS
    for chunk in range(CHUNKS):

        def multiply(group, _):
            found = []
            for u in range(UNROLL):
                at = chunk * segment + (group * UNROLL + u) * 2
                one, two = terms_ref[at], terms_ref[at + 1]
                lhs = jnp.concatenate([blocks[one & MASK], blocks[two & MASK]], axis=1)
                rhs = jnp.concatenate([blocks[(one >> BITS) & MASK], blocks[(two >> BITS) & MASK]], axis=0)
                found.append(((one >> (2 * BITS)) & OUT_MASK, jnp.dot(lhs, rhs, preferred_element_type=jnp.float32)))
            for at, value in found:
                sums[at] += value
            return 0

        lax.fori_loop(0, count_ref[stage * CHUNKS + chunk], multiply, 0)
        if final:
            span = pl.ds(chunk * part, part)
            pltpu.make_async_copy(sums.at[span], out_ref.at[span], sem).start()
    if final:
        pltpu.make_async_copy(sums, out_ref, sem).wait()


def after_all(arrays, tokens):
    count = len(arrays)
    return list(pl.pallas_call(
        lambda *refs: None,
        out_shape=[jax.ShapeDtypeStruct(a.shape, a.dtype) for a in arrays],
        in_specs=[ANY] * (count + len(tokens)),
        out_specs=[ANY] * count,
        input_output_aliases={n: n for n in range(count)},
        compiler_params=SMALL,
        cost_estimate=quick(1),
        name="after_all",
    )(*arrays, *tokens))


def rows_of(arrays, place, step, tokens, spans):
    both = step == 0 and len(arrays) == 2
    shape = arrays[0].shape[1:]

    def kernel(place_ref, *refs):
        given, given_out, sem = refs[: len(arrays)], refs[len(arrays) + len(tokens) : -1], refs[-1]

        def copies(go):
            for target, (start, stop) in zip(given_out, spans):
                rows = stop - start
                if both or len(given) == 1:
                    for n, source in enumerate(given):
                        go(pltpu.make_async_copy(source.at[pl.ds(start, rows)], target.at[pl.ds(n * rows, rows)], sem))
                    continue
                for wanted, source in ((place_ref[0] >= step, given[0]), (place_ref[0] < step, given[1])):

                    @pl.when(wanted)
                    def _(source=source, target=target, start=start, rows=rows):
                        go(pltpu.make_async_copy(source.at[pl.ds(start, rows)], target, sem))

        copies(lambda c: c.start())
        copies(lambda c: c.wait())

    return list(pl.pallas_call(
        kernel,
        out_shape=[
            jax.ShapeDtypeStruct(((2 if both else 1) * (stop - start), *shape), arrays[0].dtype)
            for start, stop in spans
        ],
        in_specs=[SMEM] + [ANY] * (len(arrays) + len(tokens)),
        out_specs=[ANY] * len(spans),
        scratch_shapes=[pltpu.SemaphoreType.DMA],
        compiler_params=SMALL,
        cost_estimate=quick(1),
        name="rows_of",
    )(place, *arrays, *tokens))


def body(block_values, block_columns, product_columns):
    row_count, own, tile, _ = block_values.shape
    dtype = block_values.dtype
    size = lax.axis_size("cols")
    last = size - 1
    slots = size * own
    wanted_slots = product_columns.shape[1]
    ext = row_count + 2 * LEAD
    out_count = row_count * wanted_slots
    segment = segment_size(row_count // CHUNKS, wanted_slots)
    first_row = lax.axis_index("rows") * row_count
    me = lax.axis_index("cols")

    plans = {stage: [] for stage in range(STAGES)}
    pieces = {stage: [] for stage in range(STAGES)}

    def keep(stage, array, source, rows, target, shift):
        plans[stage].append((source, rows, target, shift))
        pieces[stage].append(array)

    def trade(array_low, array_high, shifts, step):
        stage = stage_of(step, last, 2)
        after, before = row_shift(array_low, -1), row_shift(array_high, 1)
        for n, shift in enumerate(shifts):
            keep(stage, after, n * LEAD, LEAD, LEAD + row_count, shift)
            keep(stage, before, n * LEAD, LEAD, 0, shift)

    edges = [(0, LEAD), (row_count - LEAD, row_count)]
    middle = (LEAD, row_count - LEAD)

    place = jnp.stack([me, first_row])
    lists = []
    state = []

    def run(stage):
        count = len(pieces[stage])
        final = stage == STAGES - 1
        given = state[:-1]
        state[:] = pl.pallas_call(
            functools.partial(stage_kernel, stage, tuple(plans[stage]), ext, size, own, segment),
            out_shape=[
                pltpu.VMEM(((2 * ext + 1) * slots, tile, tile), dtype),
                pltpu.VMEM((out_count, tile, tile), jnp.float32),
                jax.ShapeDtypeStruct((out_count, tile, tile), jnp.float32)
                if final
                else jax.ShapeDtypeStruct((1,), jnp.int32),
            ],
            in_specs=[SMEM, SMEM, HBM] + [HBM] * count + [VMEM] * len(given),
            out_specs=[VMEM, VMEM, HBM if final else SMEM],
            input_output_aliases={3 + count + n: n for n in range(len(given))},
            scratch_shapes=[
                pltpu.SemaphoreType.DMA,
                pltpu.SMEM((CHUNKS * segment,), jnp.int32),
                pltpu.SemaphoreType.DMA,
            ],
            compiler_params=pltpu.CompilerParams(vmem_limit_bytes=4 << 20),
            cost_estimate=quick(WEIGHTS[stage]),
            name=f"stage_{stage}",
        )(place, *lists, *pieces[stage], *given)
        return state[-1]

    moving = [block_values, block_values]
    for step in range(1, size):
        ups, downs = up_pairs(size, step), down_pairs(size, step)
        if step == last and step > 1:
            arrived = [lax.ppermute(array, "cols", ups + downs) for array in parts]
            arrived[:2] = after_all(arrived[:2], [state[-1]])
            for array, (start, stop), edge in zip(arrived, [*edges, middle], (0, 0, 1)):
                keep(stage_of(step, last, edge), array, 0, stop - start, LEAD + start, (step,))
            trade(arrived[0], arrived[1], ((step,),), step)
            break
        if len(moving) == 2:
            moving = [lax.ppermute(array, "cols", pairs) for array, pairs in zip(moving, (ups, downs))]
        else:
            moving = [lax.ppermute(moving[0], "cols", ups + downs)]
        if step == 1:
            keep(0, block_values, 0, row_count, LEAD, 0)
            devices = size * lax.axis_size("rows")
            spread = jnp.pad(block_columns.T.reshape(-1), (0, TABLE - own * row_count))
            spread = jnp.broadcast_to(spread.reshape(1, 8, TABLE // 8), (devices, 8, TABLE // 8))
            tables = lax.all_to_all(spread, ("rows", "cols"), 0, 0, tiled=True).reshape(-1)
            trade(*rows_of([block_values], place, 0, [], edges), (0,), 0)
            moving = after_all(moving, [tables, *pieces[0][1:]])
            terms, counts = pl.pallas_call(
                functools.partial(
                    list_kernel, row_count, own, wanted_slots, size, row_count * lax.axis_size("rows")
                ),
                out_shape=[
                    jax.ShapeDtypeStruct(((STAGES * CHUNKS + 2) * segment,), jnp.int32),
                    jax.ShapeDtypeStruct((STAGES * CHUNKS,), jnp.int32),
                ],
                in_specs=[SMEM, SMEM, HBM],
                out_specs=[SMEM] * 2,
                scratch_shapes=[
                    pltpu.SMEM((ext * WIDE,), jnp.int32),
                    pltpu.SMEM(((ABSENT + 1) * CHUNKS,), jnp.int32),
                    pltpu.SMEM((3 * size * TABLE,), jnp.int32),
                    pltpu.SemaphoreType.DMA,
                ],
                compiler_params=SMALL,
                cost_estimate=quick(LIST_WEIGHT),
                name="lists",
            )(place, product_columns.T, tables)
            lists = [counts, terms]
        elif len(moving) == 2 and 2 * step > last:
            pass
        else:
            moving = after_all(moving, [])
        stage = stage_of(step, last, 0)
        shifts = (-step, step) if len(moving) == 2 else ((step,),)
        for array, shift in zip(moving, shifts):
            keep(stage, array, 0, row_count, LEAD, shift)
        if step + 1 == last:
            parts = rows_of(moving, place, step, [counts], [*edges, middle])
            trade(parts[0], parts[1], ((step,),), step)
            run(0)
            run(1)
        elif 2 * step > last:
            if len(moving) == 2:
                moving = rows_of(moving, place, step, [], [(0, row_count)])
            trade(*rows_of(moving, place, step, [], edges), ((step,),), step)
        else:
            trade(*rows_of(moving, place, 0, [], edges), (-step, step), step)
    for stage in range(2, STAGES):
        run(stage)
    return state[-1].reshape(row_count, wanted_slots, tile, tile)


def solution(mesh):
    placed = (
        P(("groups", "rows"), "cols", None, None),
        P(("groups", "rows"), "cols"),
        P(("groups", "rows"), "cols"),
    )
    return jax.shard_map(
        body,
        mesh=mesh,
        in_specs=placed,
        out_specs=P(("groups", "rows"), "cols", None, None),
        check_vma=False,
    )
```

```python
import functools

import jax
import jax.numpy as jnp
from jax import lax
from jax.experimental import pallas as pl
from jax.experimental.pallas import tpu as pltpu
from jax.sharding import PartitionSpec as P

W = 10
LEAD = W - 1
SPAN = 2 * W - 1
WIDE = 4 * W
UNROLL = 16
BITS = 10
MASK = (1 << BITS) - 1
OUT_MASK = 127
STAGE_BIT = 27
STAGES = 6
ABSENT = 7
CHUNKS = 4
TABLE = 1024
WEIGHTS = {0: 1, 1: 1, 2: 1, 3: 1, 4: 1 << 32, 5: 1}
LIST_WEIGHT = 1
EARLY = 1 << 34

SMEM = pl.BlockSpec(memory_space=pltpu.SMEM)
VMEM = pl.BlockSpec(memory_space=pltpu.VMEM)
HBM = pl.BlockSpec(memory_space=pltpu.HBM)
ANY = pl.BlockSpec(memory_space=pl.ANY)
SMALL = pltpu.CompilerParams(vmem_limit_bytes=1 << 20)


LOW, HIGH, MIDDLE, AFTER, BEFORE = range(5)


def stage_of(step, last, kind):
    if step == last and step > 1:
        return {LOW: 2, HIGH: 3, MIDDLE: 4, AFTER: 3, BEFORE: 5}[kind]
    if kind in (AFTER, BEFORE):
        return 0 if step == 0 else 2 if step == last - 1 else 1
    return 0 if step <= 1 else 1


def quick(weight):
    return pl.CostEstimate(flops=weight, bytes_accessed=weight, transcendentals=0)


def up_pairs(size, step):
    return [(i, i + 1) for i in range(step - 1, size - 1)]


def down_pairs(size, step):
    return [(i + 1, i) for i in range(size - step)]


def row_shift(array, by):
    size = lax.axis_size("rows")
    return lax.ppermute(array, "rows", [(i, i + by) for i in range(size) if 0 <= i + by < size])


def segment_size(part_rows, slot_count):
    most = part_rows * (slot_count * (SPAN + 1) - slot_count * (slot_count - 1) // 2) + 4 * UNROLL
    return -(-most // 256) * 256


def list_kernel(
    row_count,
    own,
    slot_count,
    size,
    total_rows,
    place_ref,
    wanted_ref,
    columns_hbm,
    count_ref,
    terms_ref,
    table_ref,
    at_ref,
    columns_ref,
    sem,
):
    me, first = place_ref[0], place_ref[1]
    slots = size * own
    ext = row_count + 2 * LEAD
    stored = ext * slots
    zero_id = 2 * stored
    part = row_count // CHUNKS
    segment = segment_size(part, slot_count)
    junk = STAGES * CHUNKS * segment
    zero_term = zero_id | (zero_id << BITS)
    spare = WIDE - 1
    absent = ABSENT << STAGE_BIT
    here = first // row_count
    holders = total_rows // row_count

    def fetch(go):
        for near in range(3):
            holder = jnp.clip(here + near - 1, 0, holders - 1)
            source = pl.ds(pl.multiple_of(holder * size * TABLE, TABLE), size * TABLE)
            go(pltpu.make_async_copy(columns_hbm.at[source], columns_ref.at[pl.ds(near * size * TABLE, size * TABLE)], sem))

    fetch(lambda c: c.start())

    def clear(e, _):
        for c in range(WIDE - 1):
            table_ref[e * WIDE + c] = absent
        return 0

    lax.fori_loop(0, ext, clear, 0)

    stages = []
    for k in range(size):
        distance = jnp.abs(k - me)
        picks = []
        for kind in range(5):
            stage = jnp.int32(0)
            for step in range(size):
                stage = jnp.where(distance == step, stage_of(step, size - 1, kind), stage)
            picks.append(stage << STAGE_BIT)
        stages.append(picks)
    fetch(lambda c: c.wait())

    def enter(e, row_id, near, local, stage):
        line = e * WIDE + LEAD
        for k in range(size):
            for s in range(own):
                column = columns_ref[local + ((near * size + k) * TABLE + s * row_count)]
                reach = column - row_id
                good = (column >= 0) & (reach >= 0) & (reach < W)
                code = (e * slots + (k * own + s)) + stage(k)
                table_ref[jnp.where(good, line + reach, spare)] = code
                low = good & (reach > 0) & (e + reach < ext)
                table_ref[jnp.where(low, line + reach * (WIDE - 1), spare)] = code + stored

    @pl.when(first > 0)
    def _():
        def enter_before(r, _):
            at = row_count - LEAD + r
            enter(r, first - LEAD + r, 0, at, lambda k: stages[k][BEFORE])
            return 0

        lax.fori_loop(0, LEAD, enter_before, 0)

    def enter_own(r, _):
        low, high = r < LEAD, r >= row_count - LEAD

        def stage(k):
            return jnp.where(low, stages[k][LOW], jnp.where(high, stages[k][HIGH], stages[k][MIDDLE]))

        enter(r + LEAD, first + r, 1, r, stage)
        return 0

    lax.fori_loop(0, row_count, enter_own, 0)

    @pl.when(first + row_count < total_rows)
    def _():
        def enter_after(r, _):
            enter(LEAD + row_count + r, first + row_count + r, 2, r, lambda k: stages[k][AFTER])
            return 0

        lax.fori_loop(0, LEAD, enter_after, 0)

    table_ref[spare] = absent

    lanes = range(CHUNKS)
    lines = ABSENT + 1
    for chunk in lanes:
        for stage in range(STAGES):
            at_ref[chunk * lines + stage] = (stage * CHUNKS + chunk) * segment

    def per_output(number, _):
        local = number // slot_count
        slot = number - local * slot_count
        rows = [chunk * part + local for chunk in lanes]
        wants = [wanted_ref[slot, row] for row in rows]
        distances = [jnp.where(want >= 0, want - first - row, SPAN) for want, row in zip(wants, rows)]
        tags = [(row * slot_count + slot) << (2 * BITS) for row in rows]
        bases = [(row + LEAD) * WIDE + LEAD for row in rows]
        rights_at = [base + d for base, d in zip(bases, distances)]
        for chunk in lanes:
            at_ref[chunk * lines + ABSENT] = junk
        for step in range(-LEAD, W):
            lefts = [table_ref[base + (max(step, 0) * WIDE + step)] for base in bases]
            rights = [table_ref[at + step * (WIDE - 1)] for at in rights_at]
            spots = [
                (jnp.maximum(left, right) >> STAGE_BIT) + chunk * lines
                for chunk, left, right in zip(lanes, lefts, rights)
            ]
            places = [at_ref[spot] for spot in spots]
            for chunk in lanes:
                terms_ref[places[chunk]] = lefts[chunk] + (rights[chunk] << BITS) + tags[chunk]
            for chunk in lanes:
                at_ref[spots[chunk]] = places[chunk] + 1
        for chunk in lanes:
            places = [at_ref[chunk * lines + stage] for stage in range(STAGES)]
            for stage in range(STAGES):
                terms_ref[places[stage]] = zero_term + tags[chunk]
                at_ref[chunk * lines + stage] = places[stage] + (places[stage] & 1)
        return 0

    lax.fori_loop(0, part * slot_count, per_output, 0)

    for stage in range(STAGES):
        for chunk in lanes:
            at = at_ref[chunk * lines + stage]
            tag = (chunk * part * slot_count) << (2 * BITS)
            for extra in range(2 * UNROLL):
                terms_ref[at + extra] = zero_term + tag
            used = at - (stage * CHUNKS + chunk) * segment
            count_ref[stage * CHUNKS + chunk] = (used + 2 * UNROLL - 1) // (2 * UNROLL)


def stage_kernel(stage, plan, ext, size, own, segment, place_ref, *refs):
    count = len(plan)
    first, final = stage == 0, stage == STAGES - 1
    count_ref, terms_hbm = refs[:2]
    pieces = refs[2 : count + 2]
    blocks, sums, out_ref, sem, terms_ref, list_sem = refs[count + (2 if first else 4) :]
    if not final:
        out_ref[0] = 0
    slots = size * own
    stored = ext * slots
    me = place_ref[0]

    def each(go):
        for piece, (source, rows, target, shift) in zip(pieces, plan):
            owner = me + (shift if not isinstance(shift, tuple) else jnp.where(me >= shift[0], -shift[0], shift[0]))

            @pl.when((owner >= 0) & (owner < size))
            def _(piece=piece, source=source, rows=rows, target=target, owner=owner):
                go(piece, source, rows, target, owner)

    shelf = blocks.reshape(blocks.shape[0] // slots, slots, *blocks.shape[1:])

    def copy(piece, source, rows, target, owner):
        return pltpu.make_async_copy(
            piece.at[pl.ds(source, rows)], shelf.at[pl.ds(target, rows), pl.ds(owner * own, own)], sem
        )

    def turn(piece, source, rows, target, owner):
        pace = max(n for n in range(1, 10) if rows % n == 0)

        def some(group, _):
            base = (target + group * pace) * slots + owner * own
            for r in range(pace):
                for s in range(own):
                    at = base + r * slots + s
                    blocks[stored + at] = blocks[at].T
            return 0

        lax.fori_loop(0, rows // pace, some, 0)

        def mirror(group, _):
            spots = [(target + group * 3 + r) * slots for r in range(3)]
            found = []
            for at in spots:
                tile, turned = blocks[at], blocks[stored + at]
                a = lax.broadcasted_iota(jnp.int32, tile.shape, 0)
                b = lax.broadcasted_iota(jnp.int32, tile.shape, 1)
                found.append(jnp.where(a <= b, tile, turned))
            for at, whole in zip(spots, found):
                blocks[at] = whole
                blocks[stored + at] = whole
            return 0

        @pl.when(owner == 0)
        def _():
            lax.fori_loop(0, rows // 3, mirror, 0)

    listing = pltpu.make_async_copy(
        terms_hbm.at[pl.ds(stage * CHUNKS * segment, CHUNKS * segment)], terms_ref, list_sem
    )
    listing.start()
    each(lambda *what: copy(*what).start())
    if first:
        blocks[2 * stored] = jnp.zeros(blocks.shape[1:], blocks.dtype)
        sums[...] = jnp.zeros_like(sums)
    each(lambda *what: copy(*what).wait())
    each(turn)
    listing.wait()

    part = sums.shape[0] // CHUNKS
    for chunk in range(CHUNKS):

        def multiply(group, _):
            found = []
            for u in range(UNROLL):
                at = chunk * segment + (group * UNROLL + u) * 2
                one, two = terms_ref[at], terms_ref[at + 1]
                lhs = jnp.concatenate([blocks[one & MASK], blocks[two & MASK]], axis=1)
                rhs = jnp.concatenate([blocks[(one >> BITS) & MASK], blocks[(two >> BITS) & MASK]], axis=0)
                found.append(((one >> (2 * BITS)) & OUT_MASK, jnp.dot(lhs, rhs, preferred_element_type=jnp.float32)))
            for at, value in found:
                sums[at] += value
            return 0

        lax.fori_loop(0, count_ref[stage * CHUNKS + chunk], multiply, 0)
        if final:
            span = pl.ds(chunk * part, part)
            pltpu.make_async_copy(sums.at[span], out_ref.at[span], sem).start()
    if final:
        pltpu.make_async_copy(sums, out_ref, sem).wait()


def after_all(arrays, tokens, weight=1):
    count = len(arrays)
    return list(pl.pallas_call(
        lambda *refs: None,
        out_shape=[jax.ShapeDtypeStruct(a.shape, a.dtype) for a in arrays],
        in_specs=[ANY] * (count + len(tokens)),
        out_specs=[ANY] * count,
        input_output_aliases={n: n for n in range(count)},
        compiler_params=SMALL,
        cost_estimate=quick(weight),
        name="after_all",
    )(*arrays, *tokens))


def rows_of(groups, place, step, tokens, wanted, weight=1):
    arrays = [array for group in groups for array in group]
    shape = arrays[0].shape[1:]
    first_of = [sum(len(g) for g in groups[:n]) for n in range(len(groups))]
    folds = [len(group) if step == 0 else 1 for group in groups]

    def kernel(place_ref, *refs):
        results, sem = refs[len(arrays) + len(tokens) : -1], refs[-1]

        def copies(go):
            for target, spans in zip(results, wanted):
                at = 0
                for group, start, stop in spans:
                    rows = stop - start
                    sources = refs[first_of[group] : first_of[group] + len(groups[group])]
                    if folds[group] == len(sources):
                        for source in sources:
                            go(pltpu.make_async_copy(source.at[pl.ds(start, rows)], target.at[pl.ds(at, rows)], sem))
                            at += rows
                        continue
                    for chosen, source in ((place_ref[0] >= step, sources[0]), (place_ref[0] < step, sources[1])):

                        @pl.when(chosen)
                        def _(source=source, target=target, start=start, rows=rows, at=at):
                            go(pltpu.make_async_copy(source.at[pl.ds(start, rows)], target.at[pl.ds(at, rows)], sem))

                    at += rows

        copies(lambda c: c.start())
        copies(lambda c: c.wait())

    return list(pl.pallas_call(
        kernel,
        out_shape=[
            jax.ShapeDtypeStruct((sum(folds[g] * (stop - start) for g, start, stop in spans), *shape), arrays[0].dtype)
            for spans in wanted
        ],
        in_specs=[SMEM] + [ANY] * (len(arrays) + len(tokens)),
        out_specs=[ANY] * len(wanted),
        scratch_shapes=[pltpu.SemaphoreType.DMA],
        compiler_params=SMALL,
        cost_estimate=quick(weight),
        name="rows_of",
    )(place, *arrays, *tokens))


def body(block_values, block_columns, product_columns):
    row_count, own, tile, _ = block_values.shape
    dtype = block_values.dtype
    size = lax.axis_size("cols")
    last = size - 1
    slots = size * own
    wanted_slots = product_columns.shape[1]
    ext = row_count + 2 * LEAD
    out_count = row_count * wanted_slots
    segment = segment_size(row_count // CHUNKS, wanted_slots)
    first_row = lax.axis_index("rows") * row_count
    me = lax.axis_index("cols")

    plans = {stage: [] for stage in range(STAGES)}
    pieces = {stage: [] for stage in range(STAGES)}

    def keep(stage, array, source, rows, target, shift):
        plans[stage].append((source, rows, target, shift))
        pieces[stage].append(array)

    def trade(array, by, shifts, step):
        kind, target = (AFTER, LEAD + row_count) if by < 0 else (BEFORE, 0)
        moved = row_shift(array, by)
        for n, shift in enumerate(shifts):
            keep(stage_of(step, last, kind), moved, n * LEAD, LEAD, target, shift)

    place = jnp.stack([me, first_row])
    state = []

    def run(stage):
        count = len(pieces[stage])
        final = stage == STAGES - 1
        given = state[:-1]
        state[:] = pl.pallas_call(
            functools.partial(stage_kernel, stage, tuple(plans[stage]), ext, size, own, segment),
            out_shape=[
                pltpu.VMEM(((2 * ext + 1) * slots, tile, tile), dtype),
                pltpu.VMEM((out_count, tile, tile), jnp.float32),
                jax.ShapeDtypeStruct((out_count, tile, tile), jnp.float32)
                if final
                else jax.ShapeDtypeStruct((1,), jnp.int32),
            ],
            in_specs=[SMEM, SMEM, HBM] + [HBM] * count + [VMEM] * len(given),
            out_specs=[VMEM, VMEM, HBM if final else SMEM],
            input_output_aliases={3 + count + n: n for n in range(len(given))},
            scratch_shapes=[
                pltpu.SemaphoreType.DMA,
                pltpu.SMEM((CHUNKS * segment,), jnp.int32),
                pltpu.SemaphoreType.DMA,
            ],
            compiler_params=pltpu.CompilerParams(vmem_limit_bytes=4 << 20),
            cost_estimate=quick(WEIGHTS[stage]),
            name=f"stage_{stage}",
        )(place, *lists, *pieces[stage], *given)
        return state[-1]

    low, high, middle = (0, LEAD), (row_count - LEAD, row_count), (LEAD, row_count - LEAD)
    keep(0, block_values, 0, row_count, LEAD, 0)
    low_rows, high_rows = rows_of([[block_values]], place, 0, [], [[(0, *low)], [(0, *high)]])
    trade(low_rows, -1, (0,), 0)
    trade(high_rows, 1, (0,), 0)

    devices = size * lax.axis_size("rows")
    spread = jnp.pad(block_columns.T.reshape(-1), (0, TABLE - own * row_count))
    spread = jnp.broadcast_to(spread.reshape(1, 8, TABLE // 8), (devices, 8, TABLE // 8))
    tables = lax.all_to_all(spread, ("rows", "cols"), 0, 0, tiled=True).reshape(-1)
    lists = pl.pallas_call(
        functools.partial(list_kernel, row_count, own, wanted_slots, size, row_count * lax.axis_size("rows")),
        out_shape=[
            jax.ShapeDtypeStruct((STAGES * CHUNKS,), jnp.int32),
            jax.ShapeDtypeStruct(((STAGES * CHUNKS + 2) * segment,), jnp.int32),
        ],
        in_specs=[SMEM, SMEM, HBM],
        out_specs=[SMEM] * 2,
        scratch_shapes=[
            pltpu.SMEM((ext * WIDE,), jnp.int32),
            pltpu.SMEM(((ABSENT + 1) * CHUNKS,), jnp.int32),
            pltpu.SMEM((3 * size * TABLE,), jnp.int32),
            pltpu.SemaphoreType.DMA,
        ],
        compiler_params=SMALL,
        cost_estimate=quick(LIST_WEIGHT),
        name="lists",
    )(place, product_columns.T, tables)

    moving = [block_values, block_values]
    for step in range(1, last):
        ups, downs = up_pairs(size, step), down_pairs(size, step)
        if 2 * (step - 1) > last and len(moving) == 2:
            moving = rows_of([moving], place, step - 1, [], [[(0, 0, row_count)]])
        pairs = [ups, downs] if len(moving) == 2 else [ups + downs]
        moving = [lax.ppermute(array, "cols", pair) for array, pair in zip(moving, pairs)]
        if step == 1:
            moving = after_all(moving, [tables, *pieces[0][-2:]])
        shifts = (-step, step) if len(moving) == 2 else ((step,),)
        for array, shift in zip(moving, shifts):
            keep(stage_of(step, last, LOW), array, 0, row_count, LEAD, shift)
        if step < last - 1:
            shifts, way = (((step,),), step) if 2 * step > last else ((-step, step), 0)
            low_rows, high_rows = rows_of([moving], place, way, [], [[(0, *low)], [(0, *high)]])
            trade(low_rows, -1, shifts, step)
            trade(high_rows, 1, shifts, step)

    step = last - 1
    parts = rows_of([moving], place, step, [run(0)], [[(0, *low)], [(0, *high)], [(0, *middle)]])
    pairs = up_pairs(size, last) + down_pairs(size, last)
    arrived = [lax.ppermute(array, "cols", pairs) for array in parts]
    trade(parts[0], -1, ((step,),), step)
    trade(parts[1], 1, ((step,),), step)
    arrived[:1] = after_all(arrived[:1], [run(1)], EARLY)
    keep(stage_of(last, last, LOW), arrived[0], 0, LEAD, LEAD, (last,))
    trade(arrived[0], -1, ((last,),), last)
    arrived[1:2] = after_all(arrived[1:2], [run(2)])
    keep(stage_of(last, last, HIGH), arrived[1], 0, LEAD, row_count, (last,))
    trade(arrived[1], 1, ((last,),), last)
    keep(stage_of(last, last, MIDDLE), arrived[2], 0, row_count - 2 * LEAD, 2 * LEAD, (last,))
    for stage in range(3, STAGES):
        run(stage)
    return state[-1].reshape(row_count, wanted_slots, tile, tile)


def solution(mesh):
    placed = (
        P(("groups", "rows"), "cols", None, None),
        P(("groups", "rows"), "cols"),
        P(("groups", "rows"), "cols"),
    )
    return jax.shard_map(
        body,
        mesh=mesh,
        in_specs=placed,
        out_specs=P(("groups", "rows"), "cols", None, None),
        check_vma=False,
    )
```

```python
import functools

import jax
import jax.numpy as jnp
from jax import lax
from jax.experimental import pallas as pl
from jax.experimental.pallas import tpu as pltpu
from jax.sharding import PartitionSpec as P

W = 10
LEAD = W - 1
SPAN = 2 * W - 1
WIDE = 4 * W
UNROLL = 16
FEW = 8
BITS = 10
MASK = (1 << BITS) - 1
OUT_MASK = 127
STAGE_BIT = 27
STAGES = 6
ABSENT = 7
CHUNKS = 4
TABLE = 1024
WEIGHTS = {0: 1, 1: 1, 2: 1, 3: 1, 4: 1 << 32, 5: 1}
LIST_WEIGHT = 1
EARLY = 1 << 34

SMEM = pl.BlockSpec(memory_space=pltpu.SMEM)
VMEM = pl.BlockSpec(memory_space=pltpu.VMEM)
HBM = pl.BlockSpec(memory_space=pltpu.HBM)
ANY = pl.BlockSpec(memory_space=pl.ANY)
SMALL = pltpu.CompilerParams(vmem_limit_bytes=1 << 20)


LOW, HIGH, MIDDLE, AFTER, BEFORE = range(5)


def stage_of(step, last, kind):
    if step == last and step > 1:
        return {LOW: 2, HIGH: 3, MIDDLE: 4, AFTER: 3, BEFORE: 5}[kind]
    if kind in (AFTER, BEFORE):
        return 0 if step == 0 else 2 if step == last - 1 else 1
    return 0 if step <= 1 else 1


def quick(weight):
    return pl.CostEstimate(flops=weight, bytes_accessed=weight, transcendentals=0)


def up_pairs(size, step):
    return [(i, i + 1) for i in range(step - 1, size - 1)]


def down_pairs(size, step):
    return [(i + 1, i) for i in range(size - step)]


def from_below(size, step):
    return tuple(i - step if i >= step else -1 for i in range(size))


def from_above(size, step):
    return tuple(i + step if i + step < size else -1 for i in range(size))


def either(one, other):
    return tuple(max(a, b) for a, b in zip(one, other))


def pick(me, values):
    found = jnp.int32(values[0])
    for i, value in enumerate(values[1:], 1):
        found = jnp.where(me == i, value, found)
    return found


def row_shift(array, by):
    size = lax.axis_size("rows")
    return lax.ppermute(array, "rows", [(i, i + by) for i in range(size) if 0 <= i + by < size])


def segment_size(part_rows, slot_count):
    most = part_rows * (slot_count * (SPAN + 1) - slot_count * (slot_count - 1) // 2) + 4 * UNROLL
    return -(-most // 256) * 256


def list_kernel(
    row_count,
    own,
    slot_count,
    size,
    total_rows,
    place_ref,
    wanted_ref,
    columns_hbm,
    count_ref,
    terms_ref,
    table_ref,
    at_ref,
    columns_ref,
    sem,
):
    me, first = place_ref[0], place_ref[1]
    slots = size * own
    ext = row_count + 2 * LEAD
    stored = ext * slots
    zero_id = 2 * stored
    part = row_count // CHUNKS
    segment = segment_size(part, slot_count)
    junk = STAGES * CHUNKS * segment
    zero_term = zero_id | (zero_id << BITS)
    spare = WIDE - 1
    absent = ABSENT << STAGE_BIT
    here = first // row_count
    holders = total_rows // row_count

    def fetch(go):
        for near in range(3):
            holder = jnp.clip(here + near - 1, 0, holders - 1)
            source = pl.ds(pl.multiple_of(holder * size * TABLE, TABLE), size * TABLE)
            go(pltpu.make_async_copy(columns_hbm.at[source], columns_ref.at[pl.ds(near * size * TABLE, size * TABLE)], sem))

    fetch(lambda c: c.start())

    def clear(e, _):
        for c in range(WIDE - 1):
            table_ref[e * WIDE + c] = absent
        return 0

    lax.fori_loop(0, ext, clear, 0)

    stages = []
    for k in range(size):
        distance = jnp.abs(k - me)
        picks = []
        for kind in range(5):
            stage = jnp.int32(0)
            for step in range(size):
                stage = jnp.where(distance == step, stage_of(step, size - 1, kind), stage)
            picks.append(stage << STAGE_BIT)
        stages.append(picks)
    fetch(lambda c: c.wait())

    def enter(e, row_id, near, local, stage):
        line = e * WIDE + LEAD
        for k in range(size):
            for s in range(own):
                column = columns_ref[local + ((near * size + k) * TABLE + s * row_count)]
                reach = column - row_id
                good = (column >= 0) & (reach >= 0) & (reach < W)
                code = (e * slots + (k * own + s)) + stage(k)
                table_ref[jnp.where(good, line + reach, spare)] = code
                low = good & (reach > 0) & (e + reach < ext)
                table_ref[jnp.where(low, line + reach * (WIDE - 1), spare)] = code + stored

    @pl.when(first > 0)
    def _():
        def enter_before(r, _):
            at = row_count - LEAD + r
            enter(r, first - LEAD + r, 0, at, lambda k: stages[k][BEFORE])
            return 0

        lax.fori_loop(0, LEAD, enter_before, 0)

    def enter_own(r, _):
        low, high = r < LEAD, r >= row_count - LEAD

        def stage(k):
            return jnp.where(low, stages[k][LOW], jnp.where(high, stages[k][HIGH], stages[k][MIDDLE]))

        enter(r + LEAD, first + r, 1, r, stage)
        return 0

    lax.fori_loop(0, row_count, enter_own, 0)

    @pl.when(first + row_count < total_rows)
    def _():
        def enter_after(r, _):
            enter(LEAD + row_count + r, first + row_count + r, 2, r, lambda k: stages[k][AFTER])
            return 0

        lax.fori_loop(0, LEAD, enter_after, 0)

    table_ref[spare] = absent

    lanes = range(CHUNKS)
    lines = ABSENT + 1
    for chunk in lanes:
        for stage in range(STAGES):
            at_ref[chunk * lines + stage] = (stage * CHUNKS + chunk) * segment

    def per_output(number, _):
        local = number // slot_count
        slot = number - local * slot_count
        rows = [chunk * part + local for chunk in lanes]
        wants = [wanted_ref[slot, row] for row in rows]
        distances = [jnp.where(want >= 0, want - first - row, SPAN) for want, row in zip(wants, rows)]
        tags = [(row * slot_count + slot) << (2 * BITS) for row in rows]
        bases = [(row + LEAD) * WIDE + LEAD for row in rows]
        rights_at = [base + d for base, d in zip(bases, distances)]
        for chunk in lanes:
            at_ref[chunk * lines + ABSENT] = junk
        for step in range(-LEAD, W):
            lefts = [table_ref[base + (max(step, 0) * WIDE + step)] for base in bases]
            rights = [table_ref[at + step * (WIDE - 1)] for at in rights_at]
            spots = [
                (jnp.maximum(left, right) >> STAGE_BIT) + chunk * lines
                for chunk, left, right in zip(lanes, lefts, rights)
            ]
            places = [at_ref[spot] for spot in spots]
            for chunk in lanes:
                terms_ref[places[chunk]] = lefts[chunk] + (rights[chunk] << BITS) + tags[chunk]
            for chunk in lanes:
                at_ref[spots[chunk]] = places[chunk] + 1
        for chunk in lanes:
            places = [at_ref[chunk * lines + stage] for stage in range(STAGES)]
            for stage in range(STAGES):
                terms_ref[places[stage]] = zero_term + tags[chunk]
                at_ref[chunk * lines + stage] = places[stage] + (places[stage] & 1)
        return 0

    lax.fori_loop(0, part * slot_count, per_output, 0)

    for stage in range(STAGES):
        for chunk in lanes:
            at = at_ref[chunk * lines + stage]
            tag = (chunk * part * slot_count) << (2 * BITS)
            for extra in range(2 * UNROLL):
                terms_ref[at + extra] = zero_term + tag
            used = at - (stage * CHUNKS + chunk) * segment
            count_ref[stage * CHUNKS + chunk] = (used + 2 * FEW - 1) // (2 * FEW)
    count_ref[STAGES * CHUNKS] = me


def stage_kernel(stage, plan, ext, size, own, segment, count_ref, terms_hbm, *refs):
    count = len(plan)
    first, final, writes = stage == 0, stage == STAGES - 1, stage >= STAGES - 2
    pieces = refs[:count]
    blocks, sums, out_ref, sem, terms_ref, list_sem = refs[count + (0 if first else 3 if final else 2) :]
    if not writes:
        out_ref[0] = 0
    slots = size * own
    stored = ext * slots
    me = count_ref[STAGES * CHUNKS]

    def each(go):
        for piece, (source, rows, target, owners) in zip(pieces, plan):
            owner = pick(me, owners)

            @pl.when(owner >= 0)
            def _(piece=piece, source=source, rows=rows, target=target, owner=owner):
                go(piece, source, rows, target, owner)

    shelf = blocks.reshape(blocks.shape[0] // slots, slots, *blocks.shape[1:])

    def copy(piece, source, rows, target, owner):
        return pltpu.make_async_copy(
            piece.at[pl.ds(source, rows)], shelf.at[pl.ds(target, rows), pl.ds(owner * own, own)], sem
        )

    def turn(piece, source, rows, target, owner):
        pace = max(n for n in range(1, 10) if rows % n == 0)

        def some(group, _):
            base = (target + group * pace) * slots + owner * own
            for r in range(pace):
                for s in range(own):
                    at = base + r * slots + s
                    blocks[stored + at] = blocks[at].T
            return 0

        lax.fori_loop(0, rows // pace, some, 0)

        def mirror(group, _):
            spots = [(target + group * 3 + r) * slots for r in range(3)]
            found = []
            for at in spots:
                tile, turned = blocks[at], blocks[stored + at]
                a = lax.broadcasted_iota(jnp.int32, tile.shape, 0)
                b = lax.broadcasted_iota(jnp.int32, tile.shape, 1)
                found.append(jnp.where(a <= b, tile, turned))
            for at, whole in zip(spots, found):
                blocks[at] = whole
                blocks[stored + at] = whole
            return 0

        @pl.when(owner == 0)
        def _():
            lax.fori_loop(0, rows // 3, mirror, 0)

    listing = pltpu.make_async_copy(
        terms_hbm.at[pl.ds(stage * CHUNKS * segment, CHUNKS * segment)], terms_ref, list_sem
    )
    listing.start()
    each(lambda *what: copy(*what).start())
    if first:
        blocks[2 * stored] = jnp.zeros(blocks.shape[1:], blocks.dtype)
        sums[...] = jnp.zeros_like(sums)
    each(lambda *what: copy(*what).wait())
    each(turn)
    listing.wait()

    def multiply(base, entries):
        found = []
        for u in range(entries):
            one, two = terms_ref[base + 2 * u], terms_ref[base + 2 * u + 1]
            lhs = jnp.concatenate([blocks[one & MASK], blocks[two & MASK]], axis=1)
            rhs = jnp.concatenate([blocks[(one >> BITS) & MASK], blocks[(two >> BITS) & MASK]], axis=0)
            found.append(((one >> (2 * BITS)) & OUT_MASK, jnp.dot(lhs, rhs, preferred_element_type=jnp.float32)))
        for at, value in found:
            sums[at] += value

    def work(chunk, _):
        amount = count_ref[stage * CHUNKS + chunk]
        many = UNROLL // FEW
        start = chunk * segment

        def group(n, _):
            multiply(start + n * (2 * UNROLL), UNROLL)
            return 0

        lax.fori_loop(0, amount // many, group, 0)

        def rest(n, _):
            multiply(start + n * (2 * FEW), FEW)
            return 0

        lax.fori_loop(amount // many * many, amount, rest, 0)
        return 0

    if not writes:
        lax.fori_loop(0, CHUNKS, work, 0)
        return
    part = sums.shape[0] // CHUNKS
    reached = -(-LEAD // ((ext - 2 * LEAD) // CHUNKS))
    spans = pl.ds(0, reached * part), pl.ds(reached * part, (CHUNKS - reached) * part)
    mine = spans[0] if final else spans[1]
    copying = pltpu.make_async_copy(sums.at[mine], out_ref.at[mine], sem)
    if final:
        lax.fori_loop(0, reached, work, 0)
        copying.start()
    else:
        lax.fori_loop(reached, CHUNKS, work, 0)
        copying.start()
        lax.fori_loop(0, reached, work, 0)
    copying.wait()


def after_all(arrays, tokens, weight=1):
    count = len(arrays)
    return list(pl.pallas_call(
        lambda *refs: None,
        out_shape=[jax.ShapeDtypeStruct(a.shape, a.dtype) for a in arrays],
        in_specs=[ANY] * (count + len(tokens)),
        out_specs=[ANY] * count,
        input_output_aliases={n: n for n in range(count)},
        compiler_params=SMALL,
        cost_estimate=quick(weight),
        name="after_all",
    )(*arrays, *tokens))


def rows_of(groups, place, choice, tokens, wanted):
    arrays = [array for group in groups for array in group]
    shape = arrays[0].shape[1:]
    first_of = [sum(len(g) for g in groups[:n]) for n in range(len(groups))]
    folds = [len(group) if choice is None else 1 for group in groups]

    def kernel(place_ref, *refs):
        results, sem = refs[len(arrays) + len(tokens) : -1], refs[-1]

        def copies(go):
            for target, spans in zip(results, wanted):
                at = 0
                for group, start, stop in spans:
                    rows = stop - start
                    sources = refs[first_of[group] : first_of[group] + len(groups[group])]
                    if folds[group] == len(sources):
                        for source in sources:
                            go(pltpu.make_async_copy(source.at[pl.ds(start, rows)], target.at[pl.ds(at, rows)], sem))
                            at += rows
                        continue
                    for n, source in enumerate(sources):

                        @pl.when(pick(place_ref[0], choice) == n)
                        def _(source=source, target=target, start=start, rows=rows, at=at):
                            go(pltpu.make_async_copy(source.at[pl.ds(start, rows)], target.at[pl.ds(at, rows)], sem))

                    at += rows

        copies(lambda c: c.start())
        copies(lambda c: c.wait())

    return list(pl.pallas_call(
        kernel,
        out_shape=[
            jax.ShapeDtypeStruct((sum(folds[g] * (stop - start) for g, start, stop in spans), *shape), arrays[0].dtype)
            for spans in wanted
        ],
        in_specs=[SMEM] + [ANY] * (len(arrays) + len(tokens)),
        out_specs=[ANY] * len(wanted),
        scratch_shapes=[pltpu.SemaphoreType.DMA],
        compiler_params=SMALL,
        cost_estimate=quick(1),
        name="rows_of",
    )(place, *arrays, *tokens))


def body(block_values, block_columns, product_columns):
    row_count, own, tile, _ = block_values.shape
    dtype = block_values.dtype
    size = lax.axis_size("cols")
    last = size - 1
    slots = size * own
    wanted_slots = product_columns.shape[1]
    ext = row_count + 2 * LEAD
    out_count = row_count * wanted_slots
    segment = segment_size(row_count // CHUNKS, wanted_slots)
    first_row = lax.axis_index("rows") * row_count
    me = lax.axis_index("cols")

    plans = {stage: [] for stage in range(STAGES)}
    pieces = {stage: [] for stage in range(STAGES)}

    def keep(stage, array, source, rows, target, owners):
        plans[stage].append((source, rows, target, owners))
        pieces[stage].append(array)

    def trade(array, by, holders, step):
        kind, target = (AFTER, LEAD + row_count) if by < 0 else (BEFORE, 0)
        moved = row_shift(array, by)
        for n, owners in enumerate(holders):
            keep(stage_of(step, last, kind), moved, n * LEAD, LEAD, target, owners)

    place = jnp.stack([me, first_row])
    state = []

    def run(stage):
        count = len(pieces[stage])
        final, writes = stage == STAGES - 1, stage >= STAGES - 2
        given = state if final else state[:2]
        state[:] = pl.pallas_call(
            functools.partial(stage_kernel, stage, tuple(plans[stage]), ext, size, own, segment),
            out_shape=[
                pltpu.VMEM(((2 * ext + 1) * slots, tile, tile), dtype),
                pltpu.VMEM((out_count, tile, tile), jnp.float32),
                jax.ShapeDtypeStruct((out_count, tile, tile), jnp.float32)
                if writes
                else jax.ShapeDtypeStruct((1,), jnp.int32),
            ],
            in_specs=[SMEM, HBM] + [HBM] * count + [VMEM, VMEM, HBM][: len(given)],
            out_specs=[VMEM, VMEM, HBM if writes else SMEM],
            input_output_aliases={2 + count + n: n for n in range(len(given))},
            scratch_shapes=[
                pltpu.SemaphoreType.DMA,
                pltpu.SMEM((CHUNKS * segment,), jnp.int32),
                pltpu.SemaphoreType.DMA,
            ],
            compiler_params=pltpu.CompilerParams(vmem_limit_bytes=4 << 20),
            cost_estimate=quick(WEIGHTS[stage]),
            name=f"stage_{stage}",
        )(*lists, *pieces[stage], *given)
        return state[-1]

    low, high, middle = (0, LEAD), (row_count - LEAD, row_count), (LEAD, row_count - LEAD)
    itself = tuple(range(size))
    keep(0, block_values, 0, row_count, LEAD, itself)
    low_rows, high_rows = rows_of([[block_values]], place, None, [], [[(0, *low)], [(0, *high)]])
    trade(low_rows, -1, (itself,), 0)
    trade(high_rows, 1, (itself,), 0)

    devices = size * lax.axis_size("rows")
    spread = jnp.pad(block_columns.T.reshape(-1), (0, TABLE - own * row_count))
    spread = jnp.broadcast_to(spread.reshape(1, 8, TABLE // 8), (devices, 8, TABLE // 8))
    tables = lax.all_to_all(spread, ("rows", "cols"), 0, 0, tiled=True).reshape(-1)
    lists = pl.pallas_call(
        functools.partial(list_kernel, row_count, own, wanted_slots, size, row_count * lax.axis_size("rows")),
        out_shape=[
            jax.ShapeDtypeStruct((STAGES * CHUNKS + 1,), jnp.int32),
            jax.ShapeDtypeStruct(((STAGES * CHUNKS + 2) * segment,), jnp.int32),
        ],
        in_specs=[SMEM, SMEM, HBM],
        out_specs=[SMEM] * 2,
        scratch_shapes=[
            pltpu.SMEM((ext * WIDE,), jnp.int32),
            pltpu.SMEM(((ABSENT + 1) * CHUNKS,), jnp.int32),
            pltpu.SMEM((3 * size * TABLE,), jnp.int32),
            pltpu.SemaphoreType.DMA,
        ],
        compiler_params=SMALL,
        cost_estimate=quick(LIST_WEIGHT),
        name="lists",
    )(place, product_columns.T, tables)

    def steps():
        if size == 4:
            yield [(0, [(0, 1), (1, 0), (2, 3), (3, 2)], (1, 0, 3, 2)), (0, [(1, 2), (2, 1)], (-1, 2, 1, -1))]
            yield [(1, [(1, 0), (2, 3)], (2, -1, -1, 1)), (0, [(1, 2), (2, 1)], (-1, 3, 0, -1))]
            return
        for step in range(1, last):
            below, above = from_below(size, step), from_above(size, step)
            ups, downs = up_pairs(size, step), down_pairs(size, step)
            if 2 * (step - 1) > last:
                yield [(0, ups + downs, either(below, above))]
            else:
                yield [(0, ups, below), (-1, downs, above)]

    moving = [block_values]
    for step, moves in enumerate(steps(), 1):
        if len(moves) < len(moving):
            moving = rows_of([moving], place, choice, [], [[(0, 0, row_count)]])
        moving = [lax.ppermute(moving[source], "cols", pairs) for source, pairs, _ in moves]
        if step == 1:
            moving = after_all(moving, [tables, *pieces[0][-2:]])
        holders = [owners for _, _, owners in moves]
        choice = tuple(max(range(len(holders)), key=lambda n: holders[n][i]) for i in range(size))
        for array, owners in zip(moving, holders):
            keep(stage_of(step, last, LOW), array, 0, row_count, LEAD, owners)
        if 2 * step > last:
            holders = [functools.reduce(either, holders)]
        if step < last - 1:
            way = choice if 2 * step > last else None
            low_rows, high_rows = rows_of([moving], place, way, [], [[(0, *low)], [(0, *high)]])
            trade(low_rows, -1, holders, step)
            trade(high_rows, 1, holders, step)

    parts = rows_of([moving], place, choice, [run(0)], [[(0, *low)], [(0, *high)], [(0, *middle)]])
    pairs = up_pairs(size, last) + down_pairs(size, last)
    arrived = [lax.ppermute(array, "cols", pairs) for array in parts]
    trade(parts[0], -1, holders, step)
    trade(parts[1], 1, holders, step)
    holders = [either(from_below(size, last), from_above(size, last))]
    arrived[:1] = after_all(arrived[:1], [run(1)], EARLY)
    keep(stage_of(last, last, LOW), arrived[0], 0, LEAD, LEAD, holders[0])
    trade(arrived[0], -1, holders, last)
    arrived[1:2] = after_all(arrived[1:2], [run(2)])
    keep(stage_of(last, last, HIGH), arrived[1], 0, LEAD, row_count, holders[0])
    trade(arrived[1], 1, holders, last)
    keep(stage_of(last, last, MIDDLE), arrived[2], 0, row_count - 2 * LEAD, 2 * LEAD, holders[0])
    for stage in range(3, STAGES):
        run(stage)
    return state[-1].reshape(row_count, wanted_slots, tile, tile)


def solution(mesh):
    placed = (
        P(("groups", "rows"), "cols", None, None),
        P(("groups", "rows"), "cols"),
        P(("groups", "rows"), "cols"),
    )
    return jax.shard_map(
        body,
        mesh=mesh,
        in_specs=placed,
        out_specs=P(("groups", "rows"), "cols", None, None),
        check_vma=False,
    )
```

```python
import functools

import jax
import jax.numpy as jnp
from jax import lax
from jax.experimental import pallas as pl
from jax.experimental.pallas import tpu as pltpu
from jax.sharding import PartitionSpec as P

W = 10
LEAD = W - 1
SPAN = 2 * W - 1
WIDE = 4 * W
UNROLL = 16
FEW = 8
BITS = 10
MASK = (1 << BITS) - 1
OUT_MASK = 127
STAGE_BIT = 27
STAGES = 6
ABSENT = 7
CHUNKS = 4
TABLE = 1024
WEIGHTS = {0: 1, 1: 1, 2: 1, 3: 1, 4: 1 << 32, 5: 1}
LIST_WEIGHT = 1 << 33
EARLY = 1 << 34

SMEM = pl.BlockSpec(memory_space=pltpu.SMEM)
VMEM = pl.BlockSpec(memory_space=pltpu.VMEM)
HBM = pl.BlockSpec(memory_space=pltpu.HBM)
ANY = pl.BlockSpec(memory_space=pl.ANY)
SMALL = pltpu.CompilerParams(vmem_limit_bytes=1 << 20)


LOW, HIGH, MIDDLE, AFTER, BEFORE = range(5)


def stage_of(step, last, kind):
    if step == last and step > 1:
        return {LOW: 2, HIGH: 3, MIDDLE: 4, AFTER: 3, BEFORE: 5}[kind]
    if kind in (AFTER, BEFORE):
        return 0 if step == 0 else 2 if step == last - 1 else 1
    return 0 if step <= 1 else 1


def quick(weight):
    return pl.CostEstimate(flops=weight, bytes_accessed=weight, transcendentals=0)


def up_pairs(size, step):
    return [(i, i + 1) for i in range(step - 1, size - 1)]


def down_pairs(size, step):
    return [(i + 1, i) for i in range(size - step)]


def from_below(size, step):
    return tuple(i - step if i >= step else -1 for i in range(size))


def from_above(size, step):
    return tuple(i + step if i + step < size else -1 for i in range(size))


def either(one, other):
    return tuple(max(a, b) for a, b in zip(one, other))


def pick(me, values):
    found = jnp.int32(values[0])
    for i, value in enumerate(values[1:], 1):
        found = jnp.where(me == i, value, found)
    return found


def row_shift(array, by, holders):
    rows, size = lax.axis_size("rows"), lax.axis_size("cols")
    cols = [c for c in range(size) if any(owners[c] >= 0 for owners in holders)]
    steps = [i for i in range(rows) if 0 <= i + by < rows]
    if len(cols) == size:
        return lax.ppermute(array, "rows", [(i, i + by) for i in steps])
    return lax.ppermute(array, ("rows", "cols"), [(i * size + c, (i + by) * size + c) for i in steps for c in cols])


def segment_size(part_rows, slot_count):
    most = part_rows * (slot_count * (SPAN + 1) - slot_count * (slot_count - 1) // 2) + 4 * UNROLL
    return -(-most // 256) * 256


def list_kernel(
    row_count,
    own,
    slot_count,
    size,
    total_rows,
    place_ref,
    wanted_ref,
    columns_hbm,
    count_ref,
    terms_ref,
    table_ref,
    at_ref,
    columns_ref,
    sem,
):
    me, first = place_ref[0], place_ref[1]
    slots = size * own
    ext = row_count + 2 * LEAD
    stored = ext * slots
    zero_id = 2 * stored
    part = row_count // CHUNKS
    segment = segment_size(part, slot_count)
    junk = STAGES * CHUNKS * segment
    zero_term = zero_id | (zero_id << BITS)
    spare = WIDE - 1
    absent = ABSENT << STAGE_BIT
    here = first // row_count
    holders = total_rows // row_count

    def fetch(go):
        for near in range(3):
            holder = jnp.clip(here + near - 1, 0, holders - 1)
            source = pl.ds(pl.multiple_of(holder * size * TABLE, TABLE), size * TABLE)
            go(pltpu.make_async_copy(columns_hbm.at[source], columns_ref.at[pl.ds(near * size * TABLE, size * TABLE)], sem))

    fetch(lambda c: c.start())

    def clear(e, _):
        for c in range(WIDE - 1):
            table_ref[e * WIDE + c] = absent
        return 0

    lax.fori_loop(0, ext, clear, 0)

    stages = []
    for k in range(size):
        distance = jnp.abs(k - me)
        picks = []
        for kind in range(5):
            stage = jnp.int32(0)
            for step in range(size):
                stage = jnp.where(distance == step, stage_of(step, size - 1, kind), stage)
            picks.append(stage << STAGE_BIT)
        stages.append(picks)
    fetch(lambda c: c.wait())

    def enter(e, row_id, near, local, stage):
        line = e * WIDE + LEAD
        for k in range(size):
            for s in range(own):
                column = columns_ref[local + ((near * size + k) * TABLE + s * row_count)]
                reach = column - row_id
                good = (column >= 0) & (reach >= 0) & (reach < W)
                code = (e * slots + (k * own + s)) + stage(k)
                table_ref[jnp.where(good, line + reach, spare)] = code
                low = good & (reach > 0) & (e + reach < ext)
                table_ref[jnp.where(low, line + reach * (WIDE - 1), spare)] = code + stored

    @pl.when(first > 0)
    def _():
        def enter_before(r, _):
            at = row_count - LEAD + r
            enter(r, first - LEAD + r, 0, at, lambda k: stages[k][BEFORE])
            return 0

        lax.fori_loop(0, LEAD, enter_before, 0)

    def enter_own(r, _):
        low, high = r < LEAD, r >= row_count - LEAD

        def stage(k):
            return jnp.where(low, stages[k][LOW], jnp.where(high, stages[k][HIGH], stages[k][MIDDLE]))

        enter(r + LEAD, first + r, 1, r, stage)
        return 0

    lax.fori_loop(0, row_count, enter_own, 0)

    @pl.when(first + row_count < total_rows)
    def _():
        def enter_after(r, _):
            enter(LEAD + row_count + r, first + row_count + r, 2, r, lambda k: stages[k][AFTER])
            return 0

        lax.fori_loop(0, LEAD, enter_after, 0)

    table_ref[spare] = absent

    lanes = range(CHUNKS)
    lines = ABSENT + 1
    for chunk in lanes:
        for stage in range(STAGES):
            at_ref[chunk * lines + stage] = (stage * CHUNKS + chunk) * segment

    def per_output(number, _):
        local = number // slot_count
        slot = number - local * slot_count
        rows = [chunk * part + local for chunk in lanes]
        wants = [wanted_ref[slot, row] for row in rows]
        distances = [jnp.where(want >= 0, want - first - row, SPAN) for want, row in zip(wants, rows)]
        tags = [(row * slot_count + slot) << (2 * BITS) for row in rows]
        bases = [(row + LEAD) * WIDE + LEAD for row in rows]
        rights_at = [base + d for base, d in zip(bases, distances)]
        for chunk in lanes:
            at_ref[chunk * lines + ABSENT] = junk
        for step in range(-LEAD, W):
            lefts = [table_ref[base + (max(step, 0) * WIDE + step)] for base in bases]
            rights = [table_ref[at + step * (WIDE - 1)] for at in rights_at]
            spots = [
                (jnp.maximum(left, right) >> STAGE_BIT) + chunk * lines
                for chunk, left, right in zip(lanes, lefts, rights)
            ]
            places = [at_ref[spot] for spot in spots]
            for chunk in lanes:
                terms_ref[places[chunk]] = lefts[chunk] + (rights[chunk] << BITS) + tags[chunk]
            for chunk in lanes:
                at_ref[spots[chunk]] = places[chunk] + 1
        for chunk in lanes:
            places = [at_ref[chunk * lines + stage] for stage in range(STAGES)]
            for stage in range(STAGES):
                terms_ref[places[stage]] = zero_term + tags[chunk]
                at_ref[chunk * lines + stage] = places[stage] + (places[stage] & 1)
        return 0

    lax.fori_loop(0, part * slot_count, per_output, 0)

    for stage in range(STAGES):
        for chunk in lanes:
            at = at_ref[chunk * lines + stage]
            tag = (chunk * part * slot_count) << (2 * BITS)
            for extra in range(2 * UNROLL):
                terms_ref[at + extra] = zero_term + tag
            used = at - (stage * CHUNKS + chunk) * segment
            count_ref[stage * CHUNKS + chunk] = (used + 2 * FEW - 1) // (2 * FEW)
    count_ref[STAGES * CHUNKS] = me


def stage_kernel(stage, plan, ext, size, own, segment, count_ref, terms_hbm, *refs):
    count = len(plan)
    first, final, writes = stage == 0, stage == STAGES - 1, stage >= STAGES - 2
    pieces = refs[:count]
    blocks, sums, out_ref, sem, terms_ref, list_sem = refs[count + (0 if first else 3 if final else 2) :]
    if not writes:
        out_ref[0] = 0
    slots = size * own
    stored = ext * slots
    me = count_ref[STAGES * CHUNKS]

    def each(go):
        for n, (piece, (source, rows, target, owners)) in enumerate(zip(pieces, plan)):
            owner = pick(me, owners)

            @pl.when(owner >= 0)
            def _(n=n, piece=piece, source=source, rows=rows, target=target, owner=owner):
                go(n, piece, source, rows, target, owner)

    shelf = blocks.reshape(blocks.shape[0] // slots, slots, *blocks.shape[1:])

    def copy(n, piece, source, rows, target, owner):
        return pltpu.make_async_copy(
            piece.at[pl.ds(source, rows)], shelf.at[pl.ds(target, rows), pl.ds(owner * own, own)], sem.at[n]
        )

    def turn(n, piece, source, rows, target, owner):
        copy(n, piece, source, rows, target, owner).wait()
        pace = max(n for n in range(1, 10) if rows % n == 0)

        def some(group, _):
            base = (target + group * pace) * slots + owner * own
            for r in range(pace):
                for s in range(own):
                    at = base + r * slots + s
                    blocks[stored + at] = blocks[at].T
            return 0

        lax.fori_loop(0, rows // pace, some, 0)

        def mirror(group, _):
            spots = [(target + group * 3 + r) * slots for r in range(3)]
            found = []
            for at in spots:
                tile, turned = blocks[at], blocks[stored + at]
                a = lax.broadcasted_iota(jnp.int32, tile.shape, 0)
                b = lax.broadcasted_iota(jnp.int32, tile.shape, 1)
                found.append(jnp.where(a <= b, tile, turned))
            for at, whole in zip(spots, found):
                blocks[at] = whole
                blocks[stored + at] = whole
            return 0

        @pl.when(owner == 0)
        def _():
            lax.fori_loop(0, rows // 3, mirror, 0)

    listing = pltpu.make_async_copy(
        terms_hbm.at[pl.ds(stage * CHUNKS * segment, CHUNKS * segment)], terms_ref, list_sem
    )
    listing.start()
    each(lambda *what: copy(*what).start())
    if first:
        blocks[2 * stored] = jnp.zeros(blocks.shape[1:], blocks.dtype)
        sums[...] = jnp.zeros_like(sums)
    each(turn)
    listing.wait()

    def multiply(base, entries):
        found = []
        for u in range(entries):
            one, two = terms_ref[base + 2 * u], terms_ref[base + 2 * u + 1]
            lhs = jnp.concatenate([blocks[one & MASK], blocks[two & MASK]], axis=1)
            rhs = jnp.concatenate([blocks[(one >> BITS) & MASK], blocks[(two >> BITS) & MASK]], axis=0)
            found.append(((one >> (2 * BITS)) & OUT_MASK, jnp.dot(lhs, rhs, preferred_element_type=jnp.float32)))
        for at, value in found:
            sums[at] += value

    def work(chunk, _):
        amount = count_ref[stage * CHUNKS + chunk]
        many = UNROLL // FEW
        start = chunk * segment

        def group(n, _):
            multiply(start + n * (2 * UNROLL), UNROLL)
            return 0

        lax.fori_loop(0, amount // many, group, 0)

        def rest(n, _):
            multiply(start + n * (2 * FEW), FEW)
            return 0

        lax.fori_loop(amount // many * many, amount, rest, 0)
        return 0

    if not writes:
        lax.fori_loop(0, CHUNKS, work, 0)
        return
    part = sums.shape[0] // CHUNKS
    reached = -(-LEAD // ((ext - 2 * LEAD) // CHUNKS))
    spans = pl.ds(0, reached * part), pl.ds(reached * part, (CHUNKS - reached) * part)
    mine = spans[0] if final else spans[1]
    copying = pltpu.make_async_copy(sums.at[mine], out_ref.at[mine], sem.at[0])
    if final:
        lax.fori_loop(0, reached, work, 0)
        copying.start()
    else:
        lax.fori_loop(reached, CHUNKS, work, 0)
        copying.start()
        lax.fori_loop(0, reached, work, 0)
    copying.wait()


def after_all(arrays, tokens, weight=1):
    count = len(arrays)
    return list(pl.pallas_call(
        lambda *refs: None,
        out_shape=[jax.ShapeDtypeStruct(a.shape, a.dtype) for a in arrays],
        in_specs=[ANY] * (count + len(tokens)),
        out_specs=[ANY] * count,
        input_output_aliases={n: n for n in range(count)},
        compiler_params=SMALL,
        cost_estimate=quick(weight),
        name="after_all",
    )(*arrays, *tokens))


def rows_of(groups, place, choice, tokens, wanted, shifts=None):
    arrays = [array for group in groups for array in group]
    shape = arrays[0].shape[1:]
    first_of = [sum(len(g) for g in groups[:n]) for n in range(len(groups))]
    folds = [len(group) if choice is None else 1 for group in groups]

    def kernel(place_ref, *refs):
        results, sem = refs[len(arrays) + len(tokens) : -1], refs[-1]

        def copies(go):
            for target, spans in zip(results, wanted):
                at = 0
                for group, start, stop in spans:
                    rows = stop - start
                    more = shifts or {}
                    sources = refs[first_of[group] : first_of[group] + len(groups[group])]
                    if folds[group] == len(sources):
                        for source in sources:
                            go(pltpu.make_async_copy(source.at[pl.ds(start, rows)], target.at[pl.ds(at, rows)], sem))
                            at += rows
                        continue
                    for n, source in enumerate(sources):

                        @pl.when(pick(place_ref[0], choice) == n)
                        def _(source=source, target=target, start=start - more.get((group, n), 0), rows=rows, at=at):
                            go(pltpu.make_async_copy(source.at[pl.ds(start, rows)], target.at[pl.ds(at, rows)], sem))

                    at += rows

        copies(lambda c: c.start())
        copies(lambda c: c.wait())

    return list(pl.pallas_call(
        kernel,
        out_shape=[
            jax.ShapeDtypeStruct((sum(folds[g] * (stop - start) for g, start, stop in spans), *shape), arrays[0].dtype)
            for spans in wanted
        ],
        in_specs=[SMEM] + [ANY] * (len(arrays) + len(tokens)),
        out_specs=[ANY] * len(wanted),
        scratch_shapes=[pltpu.SemaphoreType.DMA],
        compiler_params=SMALL,
        cost_estimate=quick(1),
        name="rows_of",
    )(place, *arrays, *tokens))


def body(block_values, block_columns, product_columns):
    row_count, own, tile, _ = block_values.shape
    dtype = block_values.dtype
    size = lax.axis_size("cols")
    last = size - 1
    slots = size * own
    wanted_slots = product_columns.shape[1]
    ext = row_count + 2 * LEAD
    out_count = row_count * wanted_slots
    segment = segment_size(row_count // CHUNKS, wanted_slots)
    first_row = lax.axis_index("rows") * row_count
    me = lax.axis_index("cols")

    plans = {stage: [] for stage in range(STAGES)}
    pieces = {stage: [] for stage in range(STAGES)}

    def keep(stage, array, source, rows, target, owners):
        plans[stage].append((source, rows, target, owners))
        pieces[stage].append(array)

    def trade(array, by, holders, step):
        kind, target = (AFTER, LEAD + row_count) if by < 0 else (BEFORE, 0)
        moved = row_shift(array, by, holders)
        for n, owners in enumerate(holders):
            keep(stage_of(step, last, kind), moved, n * LEAD, LEAD, target, owners)

    place = jnp.stack([me, first_row])
    state = []

    def run(stage):
        count = len(pieces[stage])
        final, writes = stage == STAGES - 1, stage >= STAGES - 2
        given = state if final else state[:2]
        state[:] = pl.pallas_call(
            functools.partial(stage_kernel, stage, tuple(plans[stage]), ext, size, own, segment),
            out_shape=[
                pltpu.VMEM(((2 * ext + 1) * slots, tile, tile), dtype),
                pltpu.VMEM((out_count, tile, tile), jnp.float32),
                jax.ShapeDtypeStruct((out_count, tile, tile), jnp.float32)
                if writes
                else jax.ShapeDtypeStruct((1,), jnp.int32),
            ],
            in_specs=[SMEM, HBM] + [HBM] * count + [VMEM, VMEM, HBM][: len(given)],
            out_specs=[VMEM, VMEM, HBM if writes else SMEM],
            input_output_aliases={2 + count + n: n for n in range(len(given))},
            scratch_shapes=[
                pltpu.SemaphoreType.DMA((count,)),
                pltpu.SMEM((CHUNKS * segment,), jnp.int32),
                pltpu.SemaphoreType.DMA,
            ],
            compiler_params=pltpu.CompilerParams(vmem_limit_bytes=4 << 20),
            cost_estimate=quick(WEIGHTS[stage]),
            name=f"stage_{stage}",
        )(*lists, *pieces[stage], *given)
        return state[-1]

    low, high, middle = (0, LEAD), (row_count - LEAD, row_count), (LEAD, row_count - LEAD)
    itself = tuple(range(size))
    keep(0, block_values, 0, row_count, LEAD, itself)
    low_rows, high_rows = rows_of([[block_values]], place, None, [], [[(0, *low)], [(0, *high)]])
    trade(low_rows, -1, (itself,), 0)
    trade(high_rows, 1, (itself,), 0)

    devices = size * lax.axis_size("rows")
    spread = jnp.pad(block_columns.T.reshape(-1), (0, TABLE - own * row_count))
    spread = jnp.broadcast_to(spread.reshape(1, 8, TABLE // 8), (devices, 8, TABLE // 8))
    tables = lax.all_to_all(spread, ("rows", "cols"), 0, 0, tiled=True).reshape(-1)
    lists = pl.pallas_call(
        functools.partial(list_kernel, row_count, own, wanted_slots, size, row_count * lax.axis_size("rows")),
        out_shape=[
            jax.ShapeDtypeStruct((STAGES * CHUNKS + 1,), jnp.int32),
            jax.ShapeDtypeStruct(((STAGES * CHUNKS + 2) * segment,), jnp.int32),
        ],
        in_specs=[SMEM, SMEM, HBM],
        out_specs=[SMEM] * 2,
        scratch_shapes=[
            pltpu.SMEM((ext * WIDE,), jnp.int32),
            pltpu.SMEM(((ABSENT + 1) * CHUNKS,), jnp.int32),
            pltpu.SMEM((3 * size * TABLE,), jnp.int32),
            pltpu.SemaphoreType.DMA,
        ],
        compiler_params=SMALL,
        cost_estimate=quick(LIST_WEIGHT),
        name="lists",
    )(place, product_columns.T, tables)

    pairs = up_pairs(size, last) + down_pairs(size, last)

    def along_line():
        moving = [block_values]
        for step in range(1, last):
            below, above = from_below(size, step), from_above(size, step)
            ups, downs = up_pairs(size, step), down_pairs(size, step)
            if 2 * (step - 1) > last:
                if len(moving) == 2:
                    moving = rows_of([moving], place, choice, [], [[(0, 0, row_count)]])
                moving, holders = [lax.ppermute(moving[0], "cols", ups + downs)], [either(below, above)]
            else:
                moving = [lax.ppermute(array, "cols", p) for array, p in ((moving[0], ups), (moving[-1], downs))]
                holders = [below, above]
            if step == 1:
                moving = after_all(moving, [tables, *pieces[0][-2:]])
            choice = tuple(0 if i >= step else 1 for i in range(size))
            for array, owners in zip(moving, holders):
                keep(stage_of(step, last, LOW), array, 0, row_count, LEAD, owners)
            if 2 * step > last:
                holders = [functools.reduce(either, holders)]
            if step < last - 1:
                way = choice if 2 * step > last else None
                low_rows, high_rows = rows_of([moving], place, way, [], [[(0, *low)], [(0, *high)]])
                trade(low_rows, -1, holders, step)
                trade(high_rows, 1, holders, step)
        parts = rows_of([moving], place, choice, [run(0)], [[(0, *low)], [(0, *high)], [(0, *middle)]])
        arrived = [lax.ppermute(array, "cols", pairs) for array in parts]
        trade(parts[0], -1, holders, last - 1)
        trade(parts[1], 1, holders, last - 1)
        return arrived, run(1)

    def along_four():
        swaps = [(0, 1), (1, 0), (2, 3), (3, 2)], [(1, 2), (2, 1)]
        near = [lax.ppermute(block_values, "cols", p) for p in swaps]
        owners = (1, 0, 3, 2), (-1, 2, 1, -1)
        near = after_all(near, [tables, *pieces[0][-2:]])
        for array, whose in zip(near, owners):
            keep(stage_of(1, last, LOW), array, 0, row_count, LEAD, whose)
        outer = lax.ppermute(near[1], "cols", [(1, 0), (2, 3)])
        keep(stage_of(2, last, LOW), outer, 0, row_count, LEAD, (2, -1, -1, 1))
        spans = low, high, middle
        inner = rows_of([near[:1]], place, None, [], [[(0, *span)] for span in spans])
        inner = [lax.ppermute(array, "cols", swaps[1]) for array in inner]
        inner[:1] = after_all(inner[:1], lists[:1])
        for array, (start, stop) in zip(inner, spans):
            keep(stage_of(2, last, LOW), array, 0, stop - start, LEAD + start, (-1, 3, 0, -1))
        arrived = [lax.ppermute(array, "cols", pairs) for array in inner]
        low_rows, high_rows = rows_of([near], place, None, [], [[(0, *low)], [(0, *high)]])
        trade(low_rows, -1, owners, 1)
        trade(high_rows, 1, owners, 1)
        low_rows, high_rows = rows_of(
            [[outer, inner[0]], [outer, inner[1]]],
            place,
            (0, 1, 1, 0),
            [run(0)],
            [[(0, *low)], [(1, *high)]],
            {(1, 1): high[0]},
        )
        trade(low_rows, -1, [(2, 3, 0, 1)], 2)
        trade(high_rows, 1, [(2, 3, 0, 1)], 2)
        return arrived, run(1)

    arrived, token = along_four() if size == 4 else along_line()
    holders = [either(from_below(size, last), from_above(size, last))]
    arrived[:1] = after_all(arrived[:1], [token], EARLY)
    keep(stage_of(last, last, LOW), arrived[0], 0, LEAD, LEAD, holders[0])
    trade(arrived[0], -1, holders, last)
    arrived[1:2] = after_all(arrived[1:2], [run(2)])
    keep(stage_of(last, last, HIGH), arrived[1], 0, LEAD, row_count, holders[0])
    trade(arrived[1], 1, holders, last)
    keep(stage_of(last, last, MIDDLE), arrived[2], 0, row_count - 2 * LEAD, 2 * LEAD, holders[0])
    for stage in range(3, STAGES):
        run(stage)
    return state[-1].reshape(row_count, wanted_slots, tile, tile)


def solution(mesh):
    placed = (
        P(("groups", "rows"), "cols", None, None),
        P(("groups", "rows"), "cols"),
        P(("groups", "rows"), "cols"),
    )
    return jax.shard_map(
        body,
        mesh=mesh,
        in_specs=placed,
        out_specs=P(("groups", "rows"), "cols", None, None),
        check_vma=False,
    )
```

```python
import functools

import jax
import jax.numpy as jnp
from jax import lax
from jax.experimental import pallas as pl
from jax.experimental.pallas import tpu as pltpu
from jax.sharding import PartitionSpec as P

W = 10
LEAD = W - 1
SPAN = 2 * W - 1
WIDE = 4 * W
UNROLL = 32
FEW = 8
BITS = 10
MASK = (1 << BITS) - 1
OUT_MASK = 127
STAGE_BIT = 27
STAGES = 6
ABSENT = 7
CHUNKS = 4
TABLE = 1024
WEIGHTS = {0: 1, 1: 1, 2: 1, 3: 1, 4: 1 << 32, 5: 1}
LIST_WEIGHT = 1 << 33
EARLY = 1 << 34

SMEM = pl.BlockSpec(memory_space=pltpu.SMEM)
VMEM = pl.BlockSpec(memory_space=pltpu.VMEM)
HBM = pl.BlockSpec(memory_space=pltpu.HBM)
ANY = pl.BlockSpec(memory_space=pl.ANY)
SMALL = pltpu.CompilerParams(vmem_limit_bytes=1 << 20)


LOW, HIGH, MIDDLE, AFTER, BEFORE = range(5)


def stage_of(step, last, kind):
    if step == last and step > 1:
        return {LOW: 2, HIGH: 3, MIDDLE: 4, AFTER: 3, BEFORE: 5}[kind]
    if kind in (AFTER, BEFORE):
        return 0 if step == 0 else 2 if step == last - 1 else 1
    return 0 if step <= 1 else 1


def quick(weight):
    return pl.CostEstimate(flops=weight, bytes_accessed=weight, transcendentals=0)


def up_pairs(size, step):
    return [(i, i + 1) for i in range(step - 1, size - 1)]


def down_pairs(size, step):
    return [(i + 1, i) for i in range(size - step)]


def from_below(size, step):
    return tuple(i - step if i >= step else -1 for i in range(size))


def from_above(size, step):
    return tuple(i + step if i + step < size else -1 for i in range(size))


def either(one, other):
    return tuple(max(a, b) for a, b in zip(one, other))


def pick(me, values):
    found = jnp.int32(values[0])
    for i, value in enumerate(values[1:], 1):
        found = jnp.where(me == i, value, found)
    return found


def row_shift(array, by, holders):
    rows, size = lax.axis_size("rows"), lax.axis_size("cols")
    cols = [c for c in range(size) if any(owners[c] >= 0 for owners in holders)]
    steps = [i for i in range(rows) if 0 <= i + by < rows]
    if len(cols) == size:
        return lax.ppermute(array, "rows", [(i, i + by) for i in steps])
    return lax.ppermute(array, ("rows", "cols"), [(i * size + c, (i + by) * size + c) for i in steps for c in cols])


def segment_size(part_rows, slot_count):
    most = part_rows * (slot_count * (SPAN + 1) - slot_count * (slot_count - 1) // 2) + 4 * FEW
    return -(-most // 256) * 256


def list_kernel(
    row_count,
    own,
    slot_count,
    size,
    total_rows,
    place_ref,
    wanted_ref,
    columns_hbm,
    count_ref,
    terms_ref,
    table_ref,
    at_ref,
    columns_ref,
    sem,
):
    me, first = place_ref[0], place_ref[1]
    slots = size * own
    ext = row_count + 2 * LEAD
    stored = ext * slots
    zero_id = 2 * stored
    part = row_count // CHUNKS
    segment = segment_size(part, slot_count)
    junk = STAGES * CHUNKS * segment
    zero_term = zero_id | (zero_id << BITS)
    spare = WIDE - 1
    absent = ABSENT << STAGE_BIT
    here = first // row_count
    holders = total_rows // row_count

    def fetch(go):
        for near in range(3):
            holder = jnp.clip(here + near - 1, 0, holders - 1)
            source = pl.ds(pl.multiple_of(holder * size * TABLE, TABLE), size * TABLE)
            go(pltpu.make_async_copy(columns_hbm.at[source], columns_ref.at[pl.ds(near * size * TABLE, size * TABLE)], sem))

    fetch(lambda c: c.start())

    def clear(e, _):
        for c in range(WIDE - 1):
            table_ref[e * WIDE + c] = absent
        return 0

    lax.fori_loop(0, ext, clear, 0)

    stages = []
    for k in range(size):
        distance = jnp.abs(k - me)
        picks = []
        for kind in range(5):
            stage = jnp.int32(0)
            for step in range(size):
                stage = jnp.where(distance == step, stage_of(step, size - 1, kind), stage)
            picks.append(stage << STAGE_BIT)
        stages.append(picks)
    fetch(lambda c: c.wait())

    def enter(e, row_id, near, local, stage):
        line = e * WIDE + LEAD
        for k in range(size):
            for s in range(own):
                column = columns_ref[local + ((near * size + k) * TABLE + s * row_count)]
                reach = column - row_id
                good = (column >= 0) & (reach >= 0) & (reach < W)
                code = (e * slots + (k * own + s)) + stage(k)
                table_ref[jnp.where(good, line + reach, spare)] = code
                low = good & (reach > 0) & (e + reach < ext)
                table_ref[jnp.where(low, line + reach * (WIDE - 1), spare)] = code + stored

    @pl.when(first > 0)
    def _():
        def enter_before(r, _):
            at = row_count - LEAD + r
            enter(r, first - LEAD + r, 0, at, lambda k: stages[k][BEFORE])
            return 0

        lax.fori_loop(0, LEAD, enter_before, 0)

    def enter_own(r, _):
        low, high = r < LEAD, r >= row_count - LEAD

        def stage(k):
            return jnp.where(low, stages[k][LOW], jnp.where(high, stages[k][HIGH], stages[k][MIDDLE]))

        enter(r + LEAD, first + r, 1, r, stage)
        return 0

    lax.fori_loop(0, row_count, enter_own, 0)

    @pl.when(first + row_count < total_rows)
    def _():
        def enter_after(r, _):
            enter(LEAD + row_count + r, first + row_count + r, 2, r, lambda k: stages[k][AFTER])
            return 0

        lax.fori_loop(0, LEAD, enter_after, 0)

    table_ref[spare] = absent

    lanes = range(CHUNKS)
    lines = ABSENT + 1
    for chunk in lanes:
        for stage in range(STAGES):
            at_ref[chunk * lines + stage] = (stage * CHUNKS + chunk) * segment

    def per_output(number, _):
        local = number // slot_count
        slot = number - local * slot_count
        rows = [chunk * part + local for chunk in lanes]
        wants = [wanted_ref[slot, row] for row in rows]
        distances = [jnp.where(want >= 0, want - first - row, SPAN) for want, row in zip(wants, rows)]
        tags = [(row * slot_count + slot) << (2 * BITS) for row in rows]
        bases = [(row + LEAD) * WIDE + LEAD for row in rows]
        rights_at = [base + d for base, d in zip(bases, distances)]
        for chunk in lanes:
            at_ref[chunk * lines + ABSENT] = junk
        for step in range(-LEAD, W):
            lefts = [table_ref[base + (max(step, 0) * WIDE + step)] for base in bases]
            rights = [table_ref[at + step * (WIDE - 1)] for at in rights_at]
            spots = [
                (jnp.maximum(left, right) >> STAGE_BIT) + chunk * lines
                for chunk, left, right in zip(lanes, lefts, rights)
            ]
            places = [at_ref[spot] for spot in spots]
            for chunk in lanes:
                terms_ref[places[chunk]] = lefts[chunk] + (rights[chunk] << BITS) + tags[chunk]
            for chunk in lanes:
                at_ref[spots[chunk]] = places[chunk] + 1
        for chunk in lanes:
            places = [at_ref[chunk * lines + stage] for stage in range(STAGES)]
            for stage in range(STAGES):
                terms_ref[places[stage]] = zero_term + tags[chunk]
                at_ref[chunk * lines + stage] = places[stage] + (places[stage] & 1)
        return 0

    lax.fori_loop(0, part * slot_count, per_output, 0)

    for stage in range(STAGES):
        for chunk in lanes:
            at = at_ref[chunk * lines + stage]
            tag = (chunk * part * slot_count) << (2 * BITS)
            for extra in range(2 * FEW):
                terms_ref[at + extra] = zero_term + tag
            used = at - (stage * CHUNKS + chunk) * segment
            count_ref[stage * CHUNKS + chunk] = (used + 2 * FEW - 1) // (2 * FEW)
    count_ref[STAGES * CHUNKS] = me


def stage_kernel(stage, plan, ext, size, own, segment, count_ref, terms_hbm, *refs):
    count = len(plan)
    first, final, writes = stage == 0, stage == STAGES - 1, stage >= STAGES - 2
    pieces = refs[:count]
    blocks, sums, out_ref, sem, terms_ref, list_sem = refs[count + (0 if first else 3 if final else 2) :]
    if not writes:
        out_ref[0] = 0
    slots = size * own
    stored = ext * slots
    me = count_ref[STAGES * CHUNKS]

    def each(go):
        for n, (piece, (source, rows, target, owners)) in enumerate(zip(pieces, plan)):
            owner = pick(me, owners)

            @pl.when(owner >= 0)
            def _(n=n, piece=piece, source=source, rows=rows, target=target, owner=owner):
                go(n, piece, source, rows, target, owner)

    shelf = blocks.reshape(blocks.shape[0] // slots, slots, *blocks.shape[1:])

    def copy(n, piece, source, rows, target, owner):
        return pltpu.make_async_copy(
            piece.at[pl.ds(source, rows)], shelf.at[pl.ds(target, rows), pl.ds(owner * own, own)], sem.at[n]
        )

    def turn(n, piece, source, rows, target, owner):
        copy(n, piece, source, rows, target, owner).wait()
        pace = max(n for n in range(1, 10) if rows % n == 0)

        def some(group, _):
            base = (target + group * pace) * slots + owner * own
            for r in range(pace):
                for s in range(own):
                    at = base + r * slots + s
                    blocks[stored + at] = blocks[at].T
            return 0

        lax.fori_loop(0, rows // pace, some, 0)

        def mirror(group, _):
            spots = [(target + group * 3 + r) * slots for r in range(3)]
            found = []
            for at in spots:
                tile, turned = blocks[at], blocks[stored + at]
                a = lax.broadcasted_iota(jnp.int32, tile.shape, 0)
                b = lax.broadcasted_iota(jnp.int32, tile.shape, 1)
                found.append(jnp.where(a <= b, tile, turned))
            for at, whole in zip(spots, found):
                blocks[at] = whole
                blocks[stored + at] = whole
            return 0

        @pl.when(owner == 0)
        def _():
            lax.fori_loop(0, rows // 3, mirror, 0)

    listing = pltpu.make_async_copy(
        terms_hbm.at[pl.ds(stage * CHUNKS * segment, CHUNKS * segment)], terms_ref, list_sem
    )
    listing.start()
    each(lambda *what: copy(*what).start())
    if first:
        blocks[2 * stored] = jnp.zeros(blocks.shape[1:], blocks.dtype)
        sums[...] = jnp.zeros_like(sums)
    each(turn)
    listing.wait()

    def multiply(base, entries):
        found = []
        for u in range(entries):
            one, two = terms_ref[base + 2 * u], terms_ref[base + 2 * u + 1]
            lhs = jnp.concatenate([blocks[one & MASK], blocks[two & MASK]], axis=1)
            rhs = jnp.concatenate([blocks[(one >> BITS) & MASK], blocks[(two >> BITS) & MASK]], axis=0)
            found.append(((one >> (2 * BITS)) & OUT_MASK, jnp.dot(lhs, rhs, preferred_element_type=jnp.float32)))
        for at, value in found:
            sums[at] += value

    def work(chunk, _):
        amount = count_ref[stage * CHUNKS + chunk]
        many = UNROLL // FEW
        start = chunk * segment

        def group(n, _):
            multiply(start + n * (2 * UNROLL), UNROLL)
            return 0

        lax.fori_loop(0, amount // many, group, 0)

        def rest(n, _):
            multiply(start + n * (2 * FEW), FEW)
            return 0

        lax.fori_loop(amount // many * many, amount, rest, 0)
        return 0

    if not writes:
        lax.fori_loop(0, CHUNKS, work, 0)
        return
    part = sums.shape[0] // CHUNKS
    reached = -(-LEAD // ((ext - 2 * LEAD) // CHUNKS))
    spans = pl.ds(0, reached * part), pl.ds(reached * part, (CHUNKS - reached) * part)
    mine = spans[0] if final else spans[1]
    copying = pltpu.make_async_copy(sums.at[mine], out_ref.at[mine], sem.at[0])
    if final:
        lax.fori_loop(0, reached, work, 0)
        copying.start()
    else:
        lax.fori_loop(reached, CHUNKS, work, 0)
        copying.start()
        lax.fori_loop(0, reached, work, 0)
    copying.wait()


def after_all(arrays, tokens, weight=1):
    count = len(arrays)
    return list(pl.pallas_call(
        lambda *refs: None,
        out_shape=[jax.ShapeDtypeStruct(a.shape, a.dtype) for a in arrays],
        in_specs=[ANY] * (count + len(tokens)),
        out_specs=[ANY] * count,
        input_output_aliases={n: n for n in range(count)},
        compiler_params=SMALL,
        cost_estimate=quick(weight),
        name="after_all",
    )(*arrays, *tokens))


def rows_of(groups, place, choice, tokens, wanted, shifts=None):
    arrays = [array for group in groups for array in group]
    shape = arrays[0].shape[1:]
    first_of = [sum(len(g) for g in groups[:n]) for n in range(len(groups))]
    folds = [len(group) if choice is None else 1 for group in groups]

    def kernel(place_ref, *refs):
        results, sem = refs[len(arrays) + len(tokens) : -1], refs[-1]

        def copies(go):
            for target, spans in zip(results, wanted):
                at = 0
                for group, start, stop in spans:
                    rows = stop - start
                    more = shifts or {}
                    sources = refs[first_of[group] : first_of[group] + len(groups[group])]
                    if folds[group] == len(sources):
                        for source in sources:
                            go(pltpu.make_async_copy(source.at[pl.ds(start, rows)], target.at[pl.ds(at, rows)], sem))
                            at += rows
                        continue
                    for n, source in enumerate(sources):

                        @pl.when(pick(place_ref[0], choice) == n)
                        def _(source=source, target=target, start=start - more.get((group, n), 0), rows=rows, at=at):
                            go(pltpu.make_async_copy(source.at[pl.ds(start, rows)], target.at[pl.ds(at, rows)], sem))

                    at += rows

        copies(lambda c: c.start())
        copies(lambda c: c.wait())

    return list(pl.pallas_call(
        kernel,
        out_shape=[
            jax.ShapeDtypeStruct((sum(folds[g] * (stop - start) for g, start, stop in spans), *shape), arrays[0].dtype)
            for spans in wanted
        ],
        in_specs=[SMEM] + [ANY] * (len(arrays) + len(tokens)),
        out_specs=[ANY] * len(wanted),
        scratch_shapes=[pltpu.SemaphoreType.DMA],
        compiler_params=SMALL,
        cost_estimate=quick(1),
        name="rows_of",
    )(place, *arrays, *tokens))


def body(block_values, block_columns, product_columns):
    row_count, own, tile, _ = block_values.shape
    dtype = block_values.dtype
    size = lax.axis_size("cols")
    last = size - 1
    slots = size * own
    wanted_slots = product_columns.shape[1]
    ext = row_count + 2 * LEAD
    out_count = row_count * wanted_slots
    segment = segment_size(row_count // CHUNKS, wanted_slots)
    first_row = lax.axis_index("rows") * row_count
    me = lax.axis_index("cols")

    plans = {stage: [] for stage in range(STAGES)}
    pieces = {stage: [] for stage in range(STAGES)}

    def keep(stage, array, source, rows, target, owners):
        plans[stage].append((source, rows, target, owners))
        pieces[stage].append(array)

    def trade(array, by, holders, step):
        kind, target = (AFTER, LEAD + row_count) if by < 0 else (BEFORE, 0)
        moved = row_shift(array, by, holders)
        for n, owners in enumerate(holders):
            keep(stage_of(step, last, kind), moved, n * LEAD, LEAD, target, owners)

    place = jnp.stack([me, first_row])
    state = []

    def run(stage):
        count = len(pieces[stage])
        final, writes = stage == STAGES - 1, stage >= STAGES - 2
        given = state if final else state[:2]
        state[:] = pl.pallas_call(
            functools.partial(stage_kernel, stage, tuple(plans[stage]), ext, size, own, segment),
            out_shape=[
                pltpu.VMEM(((2 * ext + 1) * slots, tile, tile), dtype),
                pltpu.VMEM((out_count, tile, tile), jnp.float32),
                jax.ShapeDtypeStruct((out_count, tile, tile), jnp.float32)
                if writes
                else jax.ShapeDtypeStruct((1,), jnp.int32),
            ],
            in_specs=[SMEM, HBM] + [HBM] * count + [VMEM, VMEM, HBM][: len(given)],
            out_specs=[VMEM, VMEM, HBM if writes else SMEM],
            input_output_aliases={2 + count + n: n for n in range(len(given))},
            scratch_shapes=[
                pltpu.SemaphoreType.DMA((count,)),
                pltpu.SMEM((CHUNKS * segment,), jnp.int32),
                pltpu.SemaphoreType.DMA,
            ],
            compiler_params=pltpu.CompilerParams(vmem_limit_bytes=4 << 20),
            cost_estimate=quick(WEIGHTS[stage]),
            name=f"stage_{stage}",
        )(*lists, *pieces[stage], *given)
        return state[-1]

    low, high, middle = (0, LEAD), (row_count - LEAD, row_count), (LEAD, row_count - LEAD)
    itself = tuple(range(size))
    keep(0, block_values, 0, row_count, LEAD, itself)
    low_rows, high_rows = rows_of([[block_values]], place, None, [], [[(0, *low)], [(0, *high)]])
    trade(low_rows, -1, (itself,), 0)
    trade(high_rows, 1, (itself,), 0)

    devices = size * lax.axis_size("rows")
    spread = jnp.pad(block_columns.T.reshape(-1), (0, TABLE - own * row_count))
    spread = jnp.broadcast_to(spread.reshape(1, 8, TABLE // 8), (devices, 8, TABLE // 8))
    tables = lax.all_to_all(spread, ("rows", "cols"), 0, 0, tiled=True).reshape(-1)
    lists = pl.pallas_call(
        functools.partial(list_kernel, row_count, own, wanted_slots, size, row_count * lax.axis_size("rows")),
        out_shape=[
            jax.ShapeDtypeStruct((STAGES * CHUNKS + 1,), jnp.int32),
            jax.ShapeDtypeStruct(((STAGES * CHUNKS + 2) * segment,), jnp.int32),
        ],
        in_specs=[SMEM, SMEM, HBM],
        out_specs=[SMEM] * 2,
        scratch_shapes=[
            pltpu.SMEM((ext * WIDE,), jnp.int32),
            pltpu.SMEM(((ABSENT + 1) * CHUNKS,), jnp.int32),
            pltpu.SMEM((3 * size * TABLE,), jnp.int32),
            pltpu.SemaphoreType.DMA,
        ],
        compiler_params=SMALL,
        cost_estimate=quick(LIST_WEIGHT),
        name="lists",
    )(place, product_columns.T, tables)

    pairs = up_pairs(size, last) + down_pairs(size, last)

    def along_line():
        moving = [block_values]
        for step in range(1, last):
            below, above = from_below(size, step), from_above(size, step)
            ups, downs = up_pairs(size, step), down_pairs(size, step)
            if 2 * (step - 1) > last:
                if len(moving) == 2:
                    moving = rows_of([moving], place, choice, [], [[(0, 0, row_count)]])
                moving, holders = [lax.ppermute(moving[0], "cols", ups + downs)], [either(below, above)]
            else:
                moving = [lax.ppermute(array, "cols", p) for array, p in ((moving[0], ups), (moving[-1], downs))]
                holders = [below, above]
            if step == 1:
                moving = after_all(moving, [tables, *pieces[0][-2:]])
            choice = tuple(0 if i >= step else 1 for i in range(size))
            for array, owners in zip(moving, holders):
                keep(stage_of(step, last, LOW), array, 0, row_count, LEAD, owners)
            if 2 * step > last:
                holders = [functools.reduce(either, holders)]
            if step < last - 1:
                way = choice if 2 * step > last else None
                low_rows, high_rows = rows_of([moving], place, way, [], [[(0, *low)], [(0, *high)]])
                trade(low_rows, -1, holders, step)
                trade(high_rows, 1, holders, step)
        parts = rows_of([moving], place, choice, [run(0)], [[(0, *low)], [(0, *high)], [(0, *middle)]])
        arrived = [lax.ppermute(array, "cols", pairs) for array in parts]
        trade(parts[0], -1, holders, last - 1)
        trade(parts[1], 1, holders, last - 1)
        return arrived, run(1)

    def along_four():
        swaps = [(0, 1), (1, 0), (2, 3), (3, 2)], [(1, 2), (2, 1)]
        near = [lax.ppermute(block_values, "cols", p) for p in swaps]
        owners = (1, 0, 3, 2), (-1, 2, 1, -1)
        near = after_all(near, [tables, *pieces[0][-2:]])
        for array, whose in zip(near, owners):
            keep(stage_of(1, last, LOW), array, 0, row_count, LEAD, whose)
        outer = lax.ppermute(near[1], "cols", [(1, 0), (2, 3)])
        keep(stage_of(2, last, LOW), outer, 0, row_count, LEAD, (2, -1, -1, 1))
        spans = low, high, middle
        inner = rows_of([near[:1]], place, None, [], [[(0, *span)] for span in spans])
        inner = [lax.ppermute(array, "cols", swaps[1]) for array in inner]
        inner[:1] = after_all(inner[:1], lists[:1])
        for array, (start, stop) in zip(inner, spans):
            keep(stage_of(2, last, LOW), array, 0, stop - start, LEAD + start, (-1, 3, 0, -1))
        arrived = [lax.ppermute(array, "cols", pairs) for array in inner]
        low_rows, high_rows = rows_of([near], place, None, [], [[(0, *low)], [(0, *high)]])
        trade(low_rows, -1, owners, 1)
        trade(high_rows, 1, owners, 1)
        low_rows, high_rows = rows_of(
            [[outer, inner[0]], [outer, inner[1]]],
            place,
            (0, 1, 1, 0),
            [run(0)],
            [[(0, *low)], [(1, *high)]],
            {(1, 1): high[0]},
        )
        trade(low_rows, -1, [(2, 3, 0, 1)], 2)
        trade(high_rows, 1, [(2, 3, 0, 1)], 2)
        return arrived, run(1)

    arrived, token = along_four() if size == 4 else along_line()
    holders = [either(from_below(size, last), from_above(size, last))]
    arrived[:1] = after_all(arrived[:1], [token], EARLY)
    keep(stage_of(last, last, LOW), arrived[0], 0, LEAD, LEAD, holders[0])
    trade(arrived[0], -1, holders, last)
    arrived[1:2] = after_all(arrived[1:2], [run(2)])
    keep(stage_of(last, last, HIGH), arrived[1], 0, LEAD, row_count, holders[0])
    trade(arrived[1], 1, holders, last)
    keep(stage_of(last, last, MIDDLE), arrived[2], 0, row_count - 2 * LEAD, 2 * LEAD, holders[0])
    for stage in range(3, STAGES):
        run(stage)
    return state[-1].reshape(row_count, wanted_slots, tile, tile)


def solution(mesh):
    placed = (
        P(("groups", "rows"), "cols", None, None),
        P(("groups", "rows"), "cols"),
        P(("groups", "rows"), "cols"),
    )
    return jax.shard_map(
        body,
        mesh=mesh,
        in_specs=placed,
        out_specs=P(("groups", "rows"), "cols", None, None),
        check_vma=False,
    )
```
